256 devices in a mesh: gx: 16 (over z, core), gy: 4 (over y), gz: 4 (over x).
Axes of the slice: x: 4, y: 4, z: 8, core: 2. Of those that a mesh axis runs over, the one named last changes fastest.
Arguments:
- x_start: float32 [32, 32, 64, 512], P(None, 'gx', 'gy', 'gz'), may hold values from -24 to 24
- labels: int32 [32, 64, 512], P('gx', 'gy', 'gz'), may hold values from 0 to 7
- conduct: float32 [8, 9], replicated, may hold values from 0.025 to 4
- electrodes: int32 [33], replicated, may hold values from 0 to 1048575
Outputs:
- lead_fields: float32 [32, 32, 64, 512], P(None, 'gx', 'gy', 'gz')
The draws below stay inside these ranges and needn't reach their ends.
All inputs are finite; a program needn't handle non-finite values.
Results may differ from the reference program's by a relative error of at most 0.0003.
Values sent between devices are 32-bit elements; how exact they have to be, the bound alone decides.
A program may use at most 64 MiB of HBM per device.

```python
import math
import jax
import jax.numpy as jnp
from jax import lax

NRHS = 32
LABELS = 8
ITERS = 3
CX = 2
CY = 16
CZ = 128
NX = 32
NY = 64
NZ = 512


def draw_labels(key, part):
    key = jax.random.fold_in(key, 23)
    table_key, key_x, key_y, key_z = jax.random.split(key, 4)
    span_x = CX + CX // 2
    span_y = CY + CY // 2
    span_z = CZ - CZ // 4
    shift_x = jax.random.randint(key_x, (), 0, span_x, jnp.int32)
    shift_y = jax.random.randint(key_y, (), 0, span_y, jnp.int32)
    shift_z = jax.random.randint(key_z, (), 0, span_z, jnp.int32)
    count_x = NX // span_x + 2
    count_y = NY // span_y + 2
    count_z = NZ // span_z + 2
    coarse = jax.random.randint(table_key, (count_x, count_y, count_z), 0, LABELS, jnp.int32)
    coarse = coarse.at[0, 0, 0].set(LABELS - 1)
    last_x = (NX - 1 + shift_x) // span_x
    last_y = (NY - 1 + shift_y) // span_y
    last_z = (NZ - 1 + shift_z) // span_z
    coarse = coarse.at[last_x, last_y, last_z].set(0)
    index_x = (jnp.arange(NX, dtype=jnp.int32) + shift_x) // span_x
    index_y = (jnp.arange(NY, dtype=jnp.int32) + shift_y) // span_y
    index_z = (jnp.arange(NZ, dtype=jnp.int32) + shift_z) // span_z
    return coarse[index_x[:, None, None], index_y[None, :, None], index_z[None, None, :]].astype(jnp.int32)


def draw_conduct(key, part):
    key = jax.random.fold_in(key, 31)
    scale_key, shape_key = jax.random.split(key)
    scale = jnp.exp(jax.random.uniform(scale_key, (LABELS, 1), jnp.float32, math.log(0.05), math.log(2.0)))
    scale = scale.at[0, 0].set(0.05).at[LABELS - 1, 0].set(2.0)
    aniso = jnp.exp(jax.random.uniform(shape_key, (LABELS, 9), jnp.float32, math.log(0.5), math.log(2.0)))
    return (scale * aniso).astype(jnp.float32)


def draw_x_start(key, part):
    key = jax.random.fold_in(key, 11)
    keys = jax.random.split(key, 6)
    shape = (NRHS, NX, NY, NZ)
    region_x = 2 * CX
    region_y = 2 * CY
    region_z = max(CZ // 2, 1)
    table_shape = (NX // region_x + 1, NY // region_y + 1, NZ // region_z + 1)
    rough_table = 0.02 + 0.98 * jax.random.randint(keys[0], table_shape, 0, 2, jnp.int32).astype(jnp.float32)
    rough_table = rough_table.at[0, 0, 0].set(1.0)
    rough_table = rough_table.at[(NX - 1) // region_x, (NY - 1) // region_y, (NZ - 1) // region_z].set(0.02)
    amp_table = jnp.exp(jax.random.uniform(keys[1], table_shape, jnp.float32, math.log(0.5), math.log(2.0)))
    index_x = jnp.arange(NX, dtype=jnp.int32) // region_x
    index_y = jnp.arange(NY, dtype=jnp.int32) // region_y
    index_z = jnp.arange(NZ, dtype=jnp.int32) // region_z
    rough = rough_table[index_x[:, None, None], index_y[None, :, None], index_z[None, None, :]]
    amp = amp_table[index_x[:, None, None], index_y[None, :, None], index_z[None, None, :]]
    freq = jax.random.randint(keys[2], (3, NRHS), 1, 5, jnp.int32).astype(jnp.float32)
    phase = jax.random.uniform(keys[3], (3, NRHS), jnp.float32, -math.pi, math.pi)
    pos_x = jnp.arange(NX, dtype=jnp.float32) / NX
    pos_y = jnp.arange(NY, dtype=jnp.float32) / NY
    pos_z = jnp.arange(NZ, dtype=jnp.float32) / NZ
    wave_x = jnp.cos(2.0 * math.pi * freq[0][:, None] * pos_x[None] + phase[0][:, None])
    wave_y = jnp.cos(2.0 * math.pi * freq[1][:, None] * pos_y[None] + phase[1][:, None])
    wave_z = jnp.cos(2.0 * math.pi * freq[2][:, None] * pos_z[None] + phase[2][:, None])
    smooth = wave_x[:, :, None, None] * wave_y[:, None, :, None] * wave_z[:, None, None, :]
    column = jnp.exp(jax.random.uniform(keys[4], (NRHS,), jnp.float32, math.log(0.3), math.log(3.0)))
    noise = jax.random.normal(keys[5], shape, jnp.float32)
    noise = jnp.clip(noise, -4.0, 4.0)
    base = amp[None] * (rough[None] * noise + (1.0 - rough[None]) * 2.0 * smooth)
    return jnp.clip(base * column[:, None, None, None], -24.0, 24.0).astype(jnp.float32)


def place_ends(values, own_key, smallest, high):
    longest = values.shape.index(max(values.shape))
    spots = []
    for shift in (0, 1):
        where = [jax.random.randint(jax.random.fold_in(own_key, axis), (), 0, length) for axis, length in enumerate(values.shape)]
        where[longest] = (where[longest] + shift) % values.shape[longest]
        spots.append(tuple(where))
    return values.at[spots[0]].set(smallest).at[spots[1]].set(high)


def setup_inputs(seed: int = 0) -> dict:
    key_list = jax.random.split(jax.random.key(seed), 5)
    x_start = draw_x_start(jax.random.fold_in(key_list[4], 71), 0)
    labels = draw_labels(jax.random.fold_in(key_list[4], 71), 0)
    conduct = draw_conduct(jax.random.fold_in(key_list[4], 71), 0)
    electrodes = place_ends(jax.random.randint(key_list[3], (NRHS + 1,), 0, NX * NY * NZ), jax.random.fold_in(key_list[3], 1), 0, (NX * NY * NZ) - 1).astype(jnp.int32)
    return {"x_start": x_start, "labels": labels, "conduct": conduct, "electrodes": electrodes}


LINKS = ((0, (1, 0, 0)), (1, (0, 1, 0)), (2, (0, 0, 1)), (3, (1, 1, 0)), (4, (1, -1, 0)), (5, (1, 0, 1)), (6, (1, 0, -1)), (7, (0, 1, 1)), (8, (0, 1, -1)))
HIGH = lax.Precision.HIGHEST

def neighbour(padded, offset, shape):
    dx, dy, dz = offset
    return padded[..., 1 + dx:1 + dx + shape[0], 1 + dy:1 + dy + shape[1], 1 + dz:1 + dz + shape[2]]

def link_weights(coef, coef_pad):
    shape = coef.shape[1:]
    result = []
    for kind, step in LINKS:
        for sign in (1, -1):
            offset = (sign * step[0], sign * step[1], sign * step[2])
            result.append((offset, 0.5 * (coef[kind] + neighbour(coef_pad[kind], offset, shape))))
    return result

def apply_links(field, padded, weights):
    shape = field.shape[-3:]
    total = jnp.zeros(field.shape, jnp.float32)
    for offset, weight in weights:
        total = total + weight * (field - neighbour(padded, offset, shape))
    return total

def gram(first, second):
    count = first.shape[0]
    return jnp.dot(first.reshape(count, -1), second.reshape(count, -1).T, precision=HIGH)

def combine(coeff, field):
    count = field.shape[0]
    return jnp.dot(coeff.T, field.reshape(count, -1), precision=HIGH).reshape(field.shape)

def spd_solve(matrix, right):
    lower = lax.linalg.cholesky(matrix)
    middle = lax.linalg.triangular_solve(lower, right, left_side=True, lower=True)
    return lax.linalg.triangular_solve(lower, middle, left_side=True, lower=True, transpose_a=True)

def reference(x_start, labels, conduct, electrodes):
    coef = jnp.moveaxis(jnp.take(conduct, labels, axis=0), -1, 0)
    coef_pad = jnp.pad(coef, ((0, 0), (1, 1), (1, 1), (1, 1)))
    weights = link_weights(coef, coef_pad)

    def operate(field):

        def single(one):
            return apply_links(one, jnp.pad(one, 1), weights)
        return lax.map(single, field)
    rows = jnp.arange(NRHS, dtype=jnp.int32)
    flat = jnp.zeros((NRHS, NX * NY * NZ), jnp.float32)
    flat = flat.at[rows, electrodes[:NRHS]].add(40.0)
    flat = flat.at[rows, jnp.broadcast_to(electrodes[NRHS], (NRHS,))].add(-40.0)
    sources = flat.reshape(NRHS, NX, NY, NZ)
    solution = x_start
    residual = sources - operate(solution)
    direction = residual
    rho = gram(residual, residual)
    for step in range(ITERS):
        image = operate(direction)
        alpha = spd_solve(gram(direction, image), rho)
        solution = solution + combine(alpha, direction)
        if step + 1 < ITERS:
            residual = residual - combine(alpha, image)
            rho_new = gram(residual, residual)
            beta = spd_solve(rho, rho_new)
            direction = residual + combine(beta, direction)
            rho = rho_new
    return solution
```

```python
import jax
import jax.numpy as jnp
from jax import lax
from jax.experimental import pallas as pl
from jax.experimental.pallas import tpu as pltpu
from jax.sharding import PartitionSpec as P

NRHS, LABELS = 32, 8
CX, CY, CZ = 2, 16, 128
GX, GY, GZ = 16, 4, 4
CELLS = CX * CY
F32 = jnp.float32
HIGH = lax.Precision.HIGHEST
MESH = pl.DeviceIdType.MESH

KINDS = {}
for kind, step in enumerate(
    ((1, 0, 0), (0, 1, 0), (0, 0, 1), (1, 1, 0), (1, -1, 0), (1, 0, 1), (1, 0, -1), (0, 1, 1), (0, 1, -1))
):
    KINDS[step] = kind
    KINDS[tuple(-s for s in step)] = kind
NEAR = sorted(KINDS)
CROSS = ((0, 0), (1, 0), (-1, 0), (0, 1), (0, -1))
FLAT = tuple(o for o in NEAR if o[2] == 0)
SIDE = tuple(o for o in NEAR if o[2] != 0)
PLANE = tuple((0, b, c) for b in range(GY) for c in range(GZ) if b or c)
LINE = tuple((2 * a, 0, 0) for a in range(1, GX // 2))
HALO_TILES = 90
LABEL_TILES = 36


def wrapped(offset):
    return (offset[0] % GX, offset[1] % GY, offset[2] % GZ)


def coordinates():
    return lax.axis_index("gx"), lax.axis_index("gy"), lax.axis_index("gz")


def device(offset):
    x, y, z = coordinates()
    dx, dy, dz = wrapped(offset)
    return (lax.rem(x + dx, GX), lax.rem(y + dy, GY), lax.rem(z + dz, GZ))


def from_slot(offset, order):
    return order.index(tuple(-o for o in offset))


def mm(a, b):
    return jnp.dot(a, b, precision=HIGH, preferred_element_type=F32)


def mm_t(a, b):
    return lax.dot_general(a, b, (((0,), (0,)), ((), ())), precision=HIGH, preferred_element_type=F32)


def mm_nt(a, b):
    return lax.dot_general(a, b, (((1,), (1,)), ((), ())), precision=HIGH, preferred_element_type=F32)


def lanes(shape):
    return lax.broadcasted_iota(jnp.int32, shape, 1)


def sublanes(shape):
    return lax.broadcasted_iota(jnp.int32, shape, 0)


def eliminate(matrix):
    tiles = [matrix[8 * g : 8 * g + 8] for g in range(4)]
    row = sublanes((8, 128))
    width = 8
    for start in range(0, NRHS, width):
        columns = [
            [jnp.broadcast_to(t[:, start + j : start + j + 1], (8, 128)) for t in tiles] for j in range(width)
        ]
        for j in range(width):
            own, inner = divmod(start + j, 8)
            scale = 1.0 / columns[j][own][inner : inner + 1]
            for which in [None] + list(range(j + 1, width)):
                target = tiles if which is None else columns[which]
                pivot = jnp.broadcast_to(target[own][inner : inner + 1] * scale, (8, 128))
                new = [t - c * pivot for t, c in zip(target, columns[j])]
                new[own] = jnp.where(row == inner, pivot, new[own])
                if which is None:
                    tiles = new
                else:
                    columns[which] = new
    return jnp.concatenate(tiles, axis=0)


def part(matrix, index):
    if index:
        matrix = pltpu.roll(matrix, 128 - 32 * index, 1)
    return matrix[:, :NRHS]


def lookup(label, conduct, kind):
    value = jnp.zeros(label.shape, F32)
    for tissue in range(LABELS):
        value = jnp.where(label == tissue, conduct[tissue, kind], value)
    return value


def kernel(
    x_ref, label_ref, conduct, electrodes, out_ref,
    f0, f1, f2, f3, f4, dirs, image, second,
    label_got, padded, rows, weights, side_weights,
    pack0, pack1, pack2, pack3, got0, got1, got2, got3, ends,
    give, plane_a, line_a, pair_a, mid_a, sum_a, plane_b, line_b, pair_b, mid_b, sum_b,
    dummy, halo_send, halo_recv, label_sem, red_send, red_recv,
):
    fields = (f0, f1, f2, f3)
    packs = (pack0, pack1, pack2, pack3)
    gots = (got0, got1, got2, got3)
    gx, gy, gz = coordinates()
    lane8 = lanes((8, 128))

    partners = list(dict.fromkeys([wrapped(o) for o in NEAR] + list(PLANE) + list(LINE)))
    barrier = pltpu.get_barrier_semaphore()
    for offset in partners:
        pl.semaphore_signal(barrier, inc=1, device_id=device(offset), device_id_type=MESH)
    pl.semaphore_wait(barrier, len(partners))

    def put(src, dst, send, recv, offset):
        pltpu.make_async_remote_copy(
            src_ref=src, dst_ref=dst, send_sem=send, recv_sem=recv,
            device_id=device(offset), device_id_type=MESH,
        ).start()

    def take(ref, sem):
        pltpu.make_async_copy(ref, ref, sem).wait()

    def label_part(ref, offset):
        dx, dy, _ = offset
        xs = {0: pl.ds(0, CX), 1: pl.ds(CX - 1, 1), -1: pl.ds(0, 1)}[dx]
        ys = {0: pl.ds(0, CY), 1: pl.ds(CY - 8, 8), -1: pl.ds(0, 8)}[dy]
        return ref.at[xs, ys]

    for slot, offset in enumerate(NEAR):
        put(label_part(label_ref, offset), label_part(label_got.at[slot], offset), label_sem.at[0], label_sem.at[1], offset)

    def send(level, chunk):
        field, pack, got = fields[level], packs[level], gots[level]
        r = pl.ds(16 * chunk, 16)
        ss, rs = halo_send.at[level, chunk], halo_recv.at[level, chunk]
        x_from, x_to = {1: CX, -1: 1}, {1: 0, -1: CX + 1}
        y_from, y_to = {1: CY, -1: 1}, {1: 0, -1: CY + 1}
        for dx in (1, -1):
            put(field.at[x_from[dx], 1 : CY + 1, r], field.at[x_to[dx], 1 : CY + 1, r], ss, rs, (dx, 0, 0))
        for slot, offset in enumerate(SIDE):
            put(pack.at[chunk], got.at[slot, chunk], ss, rs, offset)
        for dy in (1, -1):
            put(field.at[1 : CX + 1, y_from[dy], r], field.at[1 : CX + 1, y_to[dy], r], ss, rs, (0, dy, 0))
        for dx in (1, -1):
            for dy in (1, -1):
                put(field.at[x_from[dx], y_from[dy], r], field.at[x_to[dx], y_to[dy], r], ss, rs, (dx, dy, 0))

    for chunk in range(2):

        def load(y, acc, chunk=chunk):
            for x in range(CX):
                tile = x_ref[pl.ds(512 * chunk + CY * x + y, 16, stride=CELLS), :]
                f0[x + 1, y + 1, 16 * chunk : 16 * chunk + 16, :] = tile
                for half in range(2):
                    spot = 32 * half + CY * x + y
                    acc = jnp.where(lane8 // 2 == spot, pltpu.roll(tile[8 * half : 8 * half + 8], 2 * spot + 1, 1), acc)
            return acc

        pack0[chunk] = lax.fori_loop(0, CY, load, jnp.zeros((8, 128), F32))
        send(0, chunk)

    take(dummy.at[pl.ds(0, LABEL_TILES)], label_sem.at[1])
    lane16 = lanes((CY, 128))
    inside = {
        (0, 1): gx < GX - 1, (0, -1): gx > 0, (1, 1): gy < GY - 1, (1, -1): gy > 0, (2, 1): gz < GZ - 1, (2, -1): gz > 0,
    }

    def block(offset, x, top):
        ref = label_ref if offset == (0, 0, 0) else label_got.at[from_slot(offset, NEAR)]
        if top is None:
            return ref[x]
        return ref[x, CY - 8 : CY] if top < 0 else ref[x, 0:8]

    def put_rows(shift, xx, dx, dy):
        x = {0: xx - 1, 1: 0, -1: CX - 1}[dx]
        value = block((dx, dy, 0), x, dy or None)
        lane = lanes(value.shape)
        if shift:
            other = block((dx, dy, shift), x, dy or None)
            other = jnp.where(inside[2, shift], other, -1)
            edge = 127 if shift == 1 else 0
            value = jnp.where(lane == edge, pltpu.roll(other, (-shift) % 128, 1), pltpu.roll(value, (-shift) % 128, 1))
        if dx:
            value = jnp.where(inside[0, dx], value, -1)
        if dy:
            value = jnp.where(inside[1, dy], value, -1)
        row = {0: 8, 1: 24, -1: 0}[dy]
        padded[shift + 1, xx, row : row + value.shape[0], :] = value

    for shift in (0, 1, -1):
        for xx in range(CX + 2):
            dx = -1 if xx == 0 else (1 if xx == CX + 1 else 0)
            put_rows(shift, xx, dx, 0)
            if dx == 0 or shift == 0:
                put_rows(shift, xx, dx, 1)
                put_rows(shift, xx, dx, -1)

    for x in range(CX):
        here = padded[1, x + 1, 8:24, :]
        own = [lookup(here, conduct, kind) for kind in range(9)]
        total = jnp.zeros((CY, 128), F32)
        for offset in NEAR:
            dx, dy, dz = offset
            there = padded[dz + 1, x + 1 + dx, 8 + dy : 24 + dy, :]
            kind = KINDS[offset]
            weight = 0.5 * (own[kind] + lookup(there, conduct, kind))
            total = total + weight
            weight = jnp.where(there >= 0, weight, 0.0)
            if dz:
                weight = pltpu.roll(weight, dz % 128, 1)
                index = 9 + 5 * (dz < 0) + CROSS.index((dx, dy))
            else:
                index = 1 + FLAT.index(offset)
            rows[index, CY * x : CY * x + CY, :] = weight
        rows[0, CY * x : CY * x + CY, :] = total

    def spread(c, carry):
        for index in range(19):
            weights[index, c] = jnp.broadcast_to(rows[index, pl.ds(c, 1), :], (8, 128))
        return carry

    lax.fori_loop(0, CELLS, spread, 0)

    pair_lane = lanes((CELLS, 128))
    keep = (pair_lane % 64) // 2 == sublanes((CELLS, 128))
    for f in range(5):
        up = jnp.broadcast_to(rows[9 + f][:, 0:1], (CELLS, 128))
        down = jnp.broadcast_to(rows[14 + f][:, 127:128], (CELLS, 128))
        both = jnp.where(keep, jnp.where(pair_lane % 2 == 1, up, down), 0.0)
        side_weights[f] = jnp.broadcast_to(jnp.sum(both, axis=0, keepdims=True), (8, 128))

    flat_base = gx * (CX * GY * CY * GZ * CZ) + gy * (CY * GZ * CZ) + gz * CZ
    row8 = sublanes((8, 128))
    wanted = []
    for g in range(4):
        tile = jnp.zeros((8, 128), jnp.int32)
        for i in range(8):
            tile = jnp.where(row8 == i, electrodes[8 * g + i], tile)
        wanted.append(tile)
    common = electrodes[NRHS]

    def operate(level, chunk):
        src, got, base = fields[level], gots[level], 16 * chunk
        dst = f4 if level == 3 else fields[level + 1]

        def sides(dx, dy):
            up = got[from_slot((dx, dy, 1), SIDE), chunk]
            down = got[from_slot((dx, dy, -1), SIDE), chunk]
            return jnp.where(lane8 % 2 == 1, up, down)

        center = sides(0, 0)
        cell_x, cell_y = (lane8 % 64) // 32, (lane8 % 32) // 2
        parts = {
            (0, 0): center,
            (1, 0): jnp.where(cell_x == 1, pltpu.roll(sides(1, 0), 32, 1), pltpu.roll(center, 96, 1)),
            (-1, 0): jnp.where(cell_x == 0, pltpu.roll(sides(-1, 0), 96, 1), pltpu.roll(center, 32, 1)),
            (0, 1): jnp.where(cell_y == 15, pltpu.roll(sides(0, 1), 30, 1), pltpu.roll(center, 126, 1)),
            (0, -1): jnp.where(cell_y == 0, pltpu.roll(sides(0, -1), 98, 1), pltpu.roll(center, 2, 1)),
        }
        end = jnp.zeros((8, 128), F32)
        for f, cross in enumerate(CROSS):
            end = end + side_weights[f] * parts[cross]
        ends[...] = end

        def body(y, acc):
            results = []
            for x in range(CX):
                c = CY * x + y
                for half in range(2):
                    r = pl.ds(base + 8 * half, 8)
                    u = {
                        (dx, dy): src[x + 1 + dx, y + 1 + dy, r, :] for dx in (-1, 0, 1) for dy in (-1, 0, 1)
                    }
                    value = weights[0, c] * u[0, 0]
                    for i, offset in enumerate(FLAT):
                        value = value - weights[1 + i, c] * u[offset[0], offset[1]]
                    up = weights[9, c] * u[0, 0]
                    down = weights[14, c] * u[0, 0]
                    for f in range(1, 5):
                        up = up + weights[9 + f, c] * u[CROSS[f]]
                        down = down + weights[14 + f, c] * u[CROSS[f]]
                    spot = 32 * half + c
                    side = pltpu.roll(ends[...], 127 - 2 * spot, 1)
                    up = jnp.where(lane8 == 0, side, up)
                    down = jnp.where(lane8 == 127, side, down)
                    value = value - pltpu.roll(up, 127, 1) - pltpu.roll(down, 1, 1)
                    if level == 0:
                        flat = flat_base + x * (GY * CY * GZ * CZ) + y * (GZ * CZ) + lane8
                        hit = jnp.where(flat == wanted[2 * chunk + half], 40.0, 0.0)
                        value = (hit - jnp.where(flat == common, 40.0, 0.0)) - value
                    if level < 3:
                        acc = jnp.where(lane8 // 2 == spot, pltpu.roll(value, 2 * spot + 1, 1), acc)
                    results.append((x, r, value))
            for x, r, value in results:
                if level == 3:
                    dst[x, y, r, :] = value
                else:
                    dst[x + 1, y + 1, r, :] = value
            return acc

        acc = lax.fori_loop(0, CY, body, jnp.zeros((8, 128), F32))
        if level < 3:
            packs[level + 1][chunk] = acc

    def arrived(level, chunk):
        take(dummy, halo_recv.at[level, chunk])

    mine = gy * GZ + gz
    chip = gx // 2

    def plane_send(value, got, index):
        give[index] = value.reshape(4, 8, 128)
        got[mine] = value.reshape(4, 8, 128)
        for offset in PLANE:
            put(give.at[index], got.at[mine], red_send.at[index, 0], red_recv.at[index, 0], offset)

    def line_send(plane, got, mid, index):
        take(plane.at[0:15], red_recv.at[index, 0])
        value = plane[0]
        for i in range(1, 16):
            value = value + plane[i]
        mid[0] = value
        got[chip] = value
        for offset in LINE:
            put(mid.at[0], got.at[chip], red_send.at[index, 1], red_recv.at[index, 1], offset)

    def pair_send(line, got, mid, index):
        take(line.at[0:7], red_recv.at[index, 1])
        value = line[0]
        for i in range(1, 8):
            value = value + line[i]
        mid[1] = value
        pltpu.make_async_remote_copy(
            src_ref=mid.at[1], dst_ref=got, send_sem=red_send.at[index, 2], recv_sem=red_recv.at[index, 2],
            device_id=(gx + 1 - 2 * lax.rem(gx, 2), gy, gz), device_id_type=MESH,
        ).start()

    def pair_take(got, mid, index):
        take(got, red_recv.at[index, 2])
        return (mid[1] + got[...]).reshape(NRHS, 128)

    def field_rows(ref, y, inner):
        o = 1 if inner else 0
        return jnp.concatenate([ref[x + o, 2 * y + j + o] for j in range(2) for x in range(CX)], axis=1)

    for level in range(2):
        for chunk in range(2):
            arrived(level, chunk)
            operate(level, chunk)
            send(level + 1, chunk)

    def gram_first(y, acc):
        both = jnp.concatenate([field_rows(f1, y, True), field_rows(f2, y, True)], axis=0)
        return acc + mm_nt(both, both)

    both = lax.fori_loop(0, CY // 2, gram_first, jnp.zeros((64, 64), F32))
    wide = jnp.concatenate([both, jnp.zeros((64, 64), F32)], axis=1)
    lane32 = lanes((NRHS, 128))
    first = jnp.where(lane32 < 64, wide[:NRHS], pltpu.roll(wide[NRHS:], 32, 1))
    first = jnp.where(lane32 < 96, first, 0.0)
    plane_send(first, plane_a, 0)

    arrived(2, 0)
    operate(2, 0)
    send(3, 0)
    line_send(plane_a, line_a, mid_a, 0)
    arrived(2, 1)
    operate(2, 1)
    send(3, 1)
    pair_send(line_a, pair_a, mid_a, 0)
    arrived(3, 0)
    operate(3, 0)
    sums = pair_take(pair_a, mid_a, 0)

    solved = eliminate(pltpu.roll(sums, 96, 1))
    alpha0 = part(solved, 3)
    turn0 = mm(part(solved, 1), alpha0)
    eye = jnp.where(sublanes((NRHS, NRHS)) == lanes((NRHS, NRHS)), 1.0, 0.0)
    beta0 = turn0 - eye
    rho1 = mm(part(sums, 0), beta0)
    mix = jnp.concatenate([turn0, -alpha0], axis=0)

    arrived(3, 1)
    operate(3, 1)

    def second_block(y, acc):
        v0, u1 = field_rows(f1, y, True), field_rows(f2, y, True)
        u2, u3 = field_rows(f3, y, True), field_rows(f4, y, False)
        top = jnp.concatenate([v0, u1, u2], axis=1)
        low = jnp.concatenate([u1, u2, u3], axis=1)
        new = mm_t(mix, jnp.concatenate([top, low], axis=0))
        p1, q1, aq1 = new[:, :512], new[:, 512:1024], new[:, 1024:]
        dirs[y] = p1
        image[y] = q1
        return acc + mm_nt(q1, jnp.concatenate([p1, q1, aq1, u1], axis=0))

    grams = lax.fori_loop(0, CY // 2, second_block, jnp.zeros((NRHS, 128), F32))
    plane_send(grams, plane_b, 1)
    line_send(plane_b, line_b, mid_b, 1)
    pair_send(line_b, pair_b, mid_b, 1)
    sums = pair_take(pair_b, mid_b, 1)

    wide_rho = jnp.concatenate([rho1, jnp.zeros((NRHS, 96), F32)], axis=1)
    solved = eliminate(jnp.where(lane32 < 64, sums, pltpu.roll(wide_rho, 64, 1)))
    alpha1 = part(solved, 2)
    turn1 = mm(part(solved, 1), alpha1)
    qq, qaq, qu = part(sums, 1), part(sums, 2), part(sums, 3)
    gram2 = mm_t(alpha1, mm(qaq, alpha1) + mm(qu, beta0) - mm(qq, turn1))
    rho2 = mm(rho1, turn1 - eye)
    solved = eliminate(jnp.concatenate([gram2, rho2, jnp.zeros((NRHS, 64), F32)], axis=1))
    alpha2 = part(solved, 1)
    last = jnp.concatenate(
        [alpha0 - mm(beta0, alpha2), alpha1 + mm(turn1, alpha2), -mm(alpha1, alpha2)], axis=0
    )

    def finish(y, carry):
        update = mm_t(last, jnp.concatenate([field_rows(f1, y, True), dirs[y], image[y]], axis=0))
        for j in range(2):
            for x in range(CX):
                piece = update[:, 128 * (2 * j + x) : 128 * (2 * j + x) + 128]
                value = f0[x + 1, 2 * y + j + 1] + piece
                out_ref[pl.ds(CY * x + 2 * y + j, NRHS, stride=CELLS), :] = value
        return carry

    lax.fori_loop(0, CY // 2, finish, 0)

    take(dummy.at[pl.ds(0, LABEL_TILES)], label_sem.at[0])
    for level in range(4):
        for chunk in range(2):
            take(dummy, halo_send.at[level, chunk])
    for index, (plane, line, pair) in enumerate(((plane_a, line_a, pair_a), (plane_b, line_b, pair_b))):
        take(plane.at[0:15], red_send.at[index, 0])
        take(line.at[0:7], red_send.at[index, 1])
        take(pair, red_send.at[index, 2])


def per_device(x_start, labels, conduct, electrodes):
    vmem = pl.BlockSpec(memory_space=pltpu.VMEM)
    smem = pl.BlockSpec(memory_space=pltpu.SMEM)
    field = pltpu.VMEM((CX + 2, CY + 2, NRHS, 128), F32)
    half = pltpu.VMEM((CY // 2, NRHS, 512), F32)
    pack = pltpu.VMEM((2, 8, 128), F32)
    got = pltpu.VMEM((10, 2, 8, 128), F32)
    reduce = [
        pltpu.VMEM((16, 4, 8, 128), F32),
        pltpu.VMEM((8, 4, 8, 128), F32),
        pltpu.VMEM((4, 8, 128), F32),
        pltpu.VMEM((2, 4, 8, 128), F32),
        pltpu.VMEM((4, 8, 128), F32),
    ]
    out = pl.pallas_call(
        kernel,
        out_shape=jax.ShapeDtypeStruct((NRHS * CELLS, 128), F32),
        in_specs=[vmem, vmem, smem, smem],
        out_specs=vmem,
        scratch_shapes=[field] * 4
        + [pltpu.VMEM((CX, CY, NRHS, 128), F32), half, half, half]
        + [
            pltpu.VMEM((18, CX, CY, 128), jnp.int32),
            pltpu.VMEM((3, CX + 2, 32, 128), jnp.int32),
            pltpu.VMEM((19, CELLS, 128), F32),
            pltpu.VMEM((19, CELLS, 8, 128), F32),
            pltpu.VMEM((5, 8, 128), F32),
        ]
        + [pack] * 4
        + [got] * 4
        + [pltpu.VMEM((8, 128), F32), pltpu.VMEM((2, 4, 8, 128), F32)]
        + reduce * 2
        + [
            pltpu.VMEM((HALO_TILES, 8, 128), F32),
            pltpu.SemaphoreType.DMA((4, 2)),
            pltpu.SemaphoreType.DMA((4, 2)),
            pltpu.SemaphoreType.DMA((2,)),
            pltpu.SemaphoreType.DMA((2, 3)),
            pltpu.SemaphoreType.DMA((2, 3)),
        ],
        compiler_params=pltpu.CompilerParams(
            collective_id=0, has_side_effects=True, vmem_limit_bytes=48 * 2**20
        ),
    )(x_start.reshape(NRHS * CELLS, 128), labels, conduct, electrodes)
    return out.reshape(x_start.shape)


def solution(mesh):
    return jax.shard_map(
        per_device,
        mesh=mesh,
        in_specs=(P(None, "gx", "gy", "gz"), P("gx", "gy", "gz"), P(), P()),
        out_specs=P(None, "gx", "gy", "gz"),
        check_vma=False,
    )
```

```python
import jax
import jax.numpy as jnp
from jax import lax
from jax.experimental import pallas as pl
from jax.experimental.pallas import tpu as pltpu
from jax.sharding import PartitionSpec as P

NRHS, LABELS = 32, 8
CX, CY, CZ = 2, 16, 128
GX, GY, GZ = 16, 4, 4
CELLS = CX * CY
F32 = jnp.float32
HIGH = lax.Precision.HIGHEST
MESH = pl.DeviceIdType.MESH

KINDS = {}
for kind, step in enumerate(
    ((1, 0, 0), (0, 1, 0), (0, 0, 1), (1, 1, 0), (1, -1, 0), (1, 0, 1), (1, 0, -1), (0, 1, 1), (0, 1, -1))
):
    KINDS[step] = kind
    KINDS[tuple(-s for s in step)] = kind
NEAR = sorted(KINDS)
CROSS = ((0, 0), (1, 0), (-1, 0), (0, 1), (0, -1))
FLAT = tuple(o for o in NEAR if o[2] == 0)
SIDE = tuple(o for o in NEAR if o[2] != 0)
PLANE = tuple((0, b, c) for b in range(GY) for c in range(GZ) if b or c)
LINE = tuple((2 * a, 0, 0) for a in range(1, GX // 2))
UNROLL = 8
GRAM = 8
SECOND = 8
FINISH = 8
HALO_TILES = 90
LABEL_TILES = 36


def wrapped(offset):
    return (offset[0] % GX, offset[1] % GY, offset[2] % GZ)


def coordinates():
    return lax.axis_index("gx"), lax.axis_index("gy"), lax.axis_index("gz")


def from_slot(offset, order):
    return order.index(tuple(-o for o in offset))


def mm(a, b):
    return jnp.dot(a, b, precision=HIGH, preferred_element_type=F32)


def mm_t(a, b):
    return lax.dot_general(a, b, (((0,), (0,)), ((), ())), precision=HIGH, preferred_element_type=F32)


def mm_nt(a, b):
    return lax.dot_general(a, b, (((1,), (1,)), ((), ())), precision=HIGH, preferred_element_type=F32)


def lanes(shape):
    return lax.broadcasted_iota(jnp.int32, shape, 1)


def sublanes(shape):
    return lax.broadcasted_iota(jnp.int32, shape, 0)


def eliminate(matrices):
    sets = [[m[8 * g : 8 * g + 8] for g in range(4)] for m in matrices]
    row = sublanes((8, 128))
    width = 8
    for start in range(0, NRHS, width):
        panels = [
            [[jnp.broadcast_to(t[:, start + j : start + j + 1], (8, 128)) for t in tiles] for j in range(width)]
            for tiles in sets
        ]
        for j in range(width):
            own, inner = divmod(start + j, 8)
            for index, columns in enumerate(panels):
                scale = 1.0 / columns[j][own][inner : inner + 1]
                for which in [None] + list(range(j + 1, width)):
                    target = sets[index] if which is None else columns[which]
                    pivot = jnp.broadcast_to(target[own][inner : inner + 1] * scale, (8, 128))
                    new = [t - c * pivot for t, c in zip(target, columns[j])]
                    new[own] = jnp.where(row == inner, pivot, new[own])
                    if which is None:
                        sets[index] = new
                    else:
                        columns[which] = new
    return [jnp.concatenate(tiles, axis=0) for tiles in sets]


def part(matrix, index):
    if index:
        matrix = pltpu.roll(matrix, 128 - 32 * index, 1)
    return matrix[:, :NRHS]


def lookup(label, conduct, kind):
    value = jnp.zeros(label.shape, F32)
    for tissue in range(LABELS):
        value = jnp.where(label == tissue, conduct[tissue, kind], value)
    return value


def kernel(
    x_in, label_in, conduct_in, electrodes_in, out_ref,
    x_ref, label_ref, conduct, electrodes, in_sem,
    f0, f1, f2, f3, f4, dirs, image,
    label_got, padded, rows, weights, side_weights,
    pack0, pack1, pack2, pack3, got0, got1, got2, got3,
    give, plane_a, line_a, pair_a, mid_a, sum_a, plane_b, line_b, pair_b, mid_b, sum_b,
    dummy, halo_send, halo_recv, label_sem, red_send, red_recv,
):
    fields = (f0, f1, f2, f3)
    packs = (pack0, pack1, pack2, pack3)
    gots = (got0, got1, got2, got3)
    gx, gy, gz = coordinates()
    lane8 = lanes((8, 128))

    copies = [
        pltpu.make_async_copy(src, dst, in_sem.at[i])
        for i, (src, dst) in enumerate(
            ((x_in, x_ref), (label_in, label_ref), (conduct_in, conduct), (electrodes_in, electrodes))
        )
    ]
    for copy in copies:
        copy.start()

    partners = list(dict.fromkeys([wrapped(o) for o in NEAR] + list(PLANE) + list(LINE)))
    along = [
        {d: (c + d) & (n - 1) if d else c for d in sorted({p[a] for p in partners} | {0})}
        for a, (c, n) in enumerate(((gx, GX), (gy, GY), (gz, GZ)))
    ]

    def device(offset):
        return tuple(table[d] for table, d in zip(along, wrapped(offset)))

    barrier = pltpu.get_barrier_semaphore()
    for offset in partners:
        pl.semaphore_signal(barrier, inc=1, device_id=device(offset), device_id_type=MESH)

    copies[0].wait()
    for chunk in range(2):

        def load(i, acc, chunk=chunk):
            for inner in range(4):
                y = 4 * i + inner
                for x in range(CX):
                    tile = x_ref[pl.ds(512 * chunk + CY * x + y, 16, stride=CELLS), :]
                    f0[x + 1, y + 1, 16 * chunk : 16 * chunk + 16, :] = tile
                    for half in range(2):
                        spot = 32 * half + CY * x + y
                        moved = pltpu.roll(tile[8 * half : 8 * half + 8], 2 * spot + 1, 1)
                        acc = jnp.where(lane8 // 2 == spot, moved, acc)
            return acc

        pack0[chunk] = lax.fori_loop(0, CY // 4, load, jnp.zeros((8, 128), F32))
    for copy in copies[1:]:
        copy.wait()
    pl.semaphore_wait(barrier, len(partners))

    def put(src, dst, send, recv, offset):
        pltpu.make_async_remote_copy(
            src_ref=src, dst_ref=dst, send_sem=send, recv_sem=recv,
            device_id=device(offset), device_id_type=MESH,
        ).start()

    def take(ref, sem):
        pltpu.make_async_copy(ref, ref, sem).wait()

    def label_part(ref, offset):
        dx, dy, _ = offset
        xs = {0: pl.ds(0, CX), 1: pl.ds(CX - 1, 1), -1: pl.ds(0, 1)}[dx]
        ys = {0: pl.ds(0, CY), 1: pl.ds(CY - 8, 8), -1: pl.ds(0, 8)}[dy]
        return ref.at[xs, ys]

    x_from, x_to = {1: CX, -1: 1}, {1: 0, -1: CX + 1}
    y_from, y_to = {1: CY, -1: 1}, {1: 0, -1: CY + 1}

    def send_far(level, chunk):
        field, r = fields[level], pl.ds(16 * chunk, 16)
        ss, rs = halo_send.at[level, chunk], halo_recv.at[level, chunk]
        for dx in (1, -1):
            put(field.at[x_from[dx], 1 : CY + 1, r], field.at[x_to[dx], 1 : CY + 1, r], ss, rs, (dx, 0, 0))

    def send_near(level, chunk):
        field, pack, got = fields[level], packs[level], gots[level]
        r = pl.ds(16 * chunk, 16)
        ss, rs = halo_send.at[level, chunk], halo_recv.at[level, chunk]
        for slot, offset in enumerate(SIDE):
            put(pack.at[chunk], got.at[slot, chunk], ss, rs, offset)
        for dy in (1, -1):
            put(field.at[1 : CX + 1, y_from[dy], r], field.at[1 : CX + 1, y_to[dy], r], ss, rs, (0, dy, 0))
        for dx in (1, -1):
            for dy in (1, -1):
                put(field.at[x_from[dx], y_from[dy], r], field.at[x_to[dx], y_to[dy], r], ss, rs, (dx, dy, 0))

    def send(level, chunk):
        send_far(level, chunk)
        send_near(level, chunk)

    send_far(0, 0)
    for slot, offset in enumerate(NEAR):
        put(label_part(label_ref, offset), label_part(label_got.at[slot], offset), label_sem.at[0], label_sem.at[1], offset)
    send_near(0, 0)
    send(0, 1)

    take(dummy.at[pl.ds(0, LABEL_TILES)], label_sem.at[1])
    lane16 = lanes((CY, 128))
    inside = {
        (0, 1): gx < GX - 1, (0, -1): gx > 0, (1, 1): gy < GY - 1, (1, -1): gy > 0, (2, 1): gz < GZ - 1, (2, -1): gz > 0,
    }

    def block(offset, x, top):
        ref = label_ref if offset == (0, 0, 0) else label_got.at[from_slot(offset, NEAR)]
        if top is None:
            return ref[x]
        return ref[x, CY - 8 : CY] if top < 0 else ref[x, 0:8]

    def put_rows(shift, xx, dx, dy):
        x = {0: xx - 1, 1: 0, -1: CX - 1}[dx]
        value = block((dx, dy, 0), x, dy or None)
        lane = lanes(value.shape)
        if shift:
            other = block((dx, dy, shift), x, dy or None)
            other = jnp.where(inside[2, shift], other, -1)
            edge = 127 if shift == 1 else 0
            value = jnp.where(lane == edge, pltpu.roll(other, (-shift) % 128, 1), pltpu.roll(value, (-shift) % 128, 1))
        if dx:
            value = jnp.where(inside[0, dx], value, -1)
        if dy:
            value = jnp.where(inside[1, dy], value, -1)
        row = {0: 8, 1: 24, -1: 0}[dy]
        padded[shift + 1, xx, row : row + value.shape[0], :] = value

    for shift in (0, 1, -1):
        for xx in range(CX + 2):
            dx = -1 if xx == 0 else (1 if xx == CX + 1 else 0)
            put_rows(shift, xx, dx, 0)
            if dx == 0 or shift == 0:
                put_rows(shift, xx, dx, 1)
                put_rows(shift, xx, dx, -1)

    for x in range(CX):
        here = padded[1, x + 1, 8:24, :]
        own = [lookup(here, conduct, kind) for kind in range(9)]
        total = jnp.zeros((CY, 128), F32)
        for offset in NEAR:
            dx, dy, dz = offset
            there = padded[dz + 1, x + 1 + dx, 8 + dy : 24 + dy, :]
            kind = KINDS[offset]
            weight = 0.5 * (own[kind] + lookup(there, conduct, kind))
            total = total + weight
            weight = jnp.where(there >= 0, weight, 0.0)
            if dz:
                weight = pltpu.roll(weight, dz % 128, 1)
                index = 9 + 5 * (dz < 0) + CROSS.index((dx, dy))
            else:
                index = 1 + FLAT.index(offset)
            rows[index, CY * x : CY * x + CY, :] = weight
        rows[0, CY * x : CY * x + CY, :] = total

    def spread(c, carry):
        for index in range(19):
            weights[index, c] = jnp.broadcast_to(rows[index, pl.ds(c, 1), :], (8, 128))
        return carry

    lax.fori_loop(0, CELLS, spread, 0)

    pair_lane = lanes((CELLS, 128))
    keep = (pair_lane % 64) // 2 == sublanes((CELLS, 128))
    for f in range(5):
        up = jnp.broadcast_to(rows[9 + f][:, 0:1], (CELLS, 128))
        down = jnp.broadcast_to(rows[14 + f][:, 127:128], (CELLS, 128))
        both = jnp.where(keep, jnp.where(pair_lane % 2 == 1, up, down), 0.0)
        side_weights[f] = jnp.broadcast_to(jnp.sum(both, axis=0, keepdims=True), (8, 128))

    flat_base = gx * (CX * GY * CY * GZ * CZ) + gy * (CY * GZ * CZ) + gz * CZ
    row8 = sublanes((8, 128))
    wanted = []
    for g in range(4):
        tile = jnp.zeros((8, 128), jnp.int32)
        for i in range(8):
            tile = jnp.where(row8 == i, electrodes[8 * g + i], tile)
        wanted.append(tile)
    common = electrodes[NRHS]

    def operate(level, chunk):
        src, got, base = fields[level], gots[level], 16 * chunk
        dst = f4 if level == 3 else fields[level + 1]

        def sides(dx, dy):
            up = got[from_slot((dx, dy, 1), SIDE), chunk]
            down = got[from_slot((dx, dy, -1), SIDE), chunk]
            return jnp.where(lane8 % 2 == 1, up, down)

        center = sides(0, 0)
        cell_x, cell_y = (lane8 % 64) // 32, (lane8 % 32) // 2
        parts = {
            (0, 0): center,
            (1, 0): jnp.where(cell_x == 1, pltpu.roll(sides(1, 0), 32, 1), pltpu.roll(center, 96, 1)),
            (-1, 0): jnp.where(cell_x == 0, pltpu.roll(sides(-1, 0), 96, 1), pltpu.roll(center, 32, 1)),
            (0, 1): jnp.where(cell_y == 15, pltpu.roll(sides(0, 1), 30, 1), pltpu.roll(center, 126, 1)),
            (0, -1): jnp.where(cell_y == 0, pltpu.roll(sides(0, -1), 98, 1), pltpu.roll(center, 2, 1)),
        }
        end = jnp.zeros((8, 128), F32)
        for f, cross in enumerate(CROSS):
            end = end + side_weights[f] * parts[cross]

        def body(i, acc):
            held, loaded, results = {}, {}, []

            def weight(index, c, key):
                if (index, key) not in held:
                    held[index, key] = weights[index, c]
                return held[index, key]

            def field(xx, inner, half):
                if (xx, inner, half) not in loaded:
                    loaded[xx, inner, half] = src[xx, UNROLL * i + inner, pl.ds(base + 8 * half, 8), :]
                return loaded[xx, inner, half]

            for inner in range(UNROLL):
                y = UNROLL * i + inner
                for x in range(CX):
                    c = CY * x + y
                    for half in range(2):
                        key = (x, inner)
                        u = {
                            (dx, dy): field(x + 1 + dx, inner + 1 + dy, half) for dx in (-1, 0, 1) for dy in (-1, 0, 1)
                        }
                        value = weight(0, c, key) * u[0, 0]
                        for k, offset in enumerate(FLAT):
                            value = value - weight(1 + k, c, key) * u[offset[0], offset[1]]
                        up = weight(9, c, key) * u[0, 0]
                        down = weight(14, c, key) * u[0, 0]
                        for f in range(1, 5):
                            up = up + weight(9 + f, c, key) * u[CROSS[f]]
                            down = down + weight(14 + f, c, key) * u[CROSS[f]]
                        spot = 32 * half + c
                        side = pltpu.roll(end, 127 - 2 * spot, 1)
                        up = jnp.where(lane8 == 0, side, up)
                        down = jnp.where(lane8 == 127, side, down)
                        value = value - pltpu.roll(up, 127, 1) - pltpu.roll(down, 1, 1)
                        if level == 0:
                            flat = flat_base + x * (GY * CY * GZ * CZ) + y * (GZ * CZ) + lane8
                            hit = jnp.where(flat == wanted[2 * chunk + half], 40.0, 0.0)
                            value = (hit - jnp.where(flat == common, 40.0, 0.0)) - value
                        if level < 3:
                            acc = jnp.where(lane8 // 2 == spot, pltpu.roll(value, 2 * spot + 1, 1), acc)
                        results.append((x, y, half, value))
            for x, y, half, value in results:
                if level == 3:
                    dst[x, y, pl.ds(base + 8 * half, 8), :] = value
                else:
                    dst[x + 1, y + 1, pl.ds(base + 8 * half, 8), :] = value
            return acc

        acc = lax.fori_loop(0, CY // UNROLL, body, jnp.zeros((8, 128), F32))
        if level < 3:
            packs[level + 1][chunk] = acc

    def arrived(level, chunk):
        take(dummy, halo_recv.at[level, chunk])

    mine = gy * GZ + gz
    chip = gx // 2

    def plane_send(value, got, index):
        spare = value[24:32]
        for g in range(3):
            tile = jnp.where(lane8 < 96, value[8 * g : 8 * g + 8], pltpu.roll(spare, 96 - 32 * g, 1))
            give[index, g] = tile
            got[mine, g] = tile
        for offset in PLANE:
            put(give.at[index], got.at[mine], red_send.at[index, 0], red_recv.at[index, 0], offset)

    def line_send(plane, got, mid, index):
        take(plane.at[0:15], red_recv.at[index, 0])
        value = plane[0]
        for i in range(1, 16):
            value = value + plane[i]
        mid[0] = value
        got[chip] = value
        for offset in LINE:
            put(mid.at[0], got.at[chip], red_send.at[index, 1], red_recv.at[index, 1], offset)

    def pair_send(line, got, mid, index):
        take(line.at[0:7], red_recv.at[index, 1])
        value = line[0]
        for i in range(1, 8):
            value = value + line[i]
        mid[1] = value
        pltpu.make_async_remote_copy(
            src_ref=mid.at[1], dst_ref=got, send_sem=red_send.at[index, 2], recv_sem=red_recv.at[index, 2],
            device_id=(gx + 1 - 2 * lax.rem(gx, 2), gy, gz), device_id_type=MESH,
        ).start()

    def pair_take(got, mid, index):
        take(got, red_recv.at[index, 2])
        tiles = [mid[1, g] + got[g] for g in range(3)]
        spare = jnp.zeros((8, 128), F32)
        for g in range(3):
            spare = jnp.where(lane8 // 32 == g, pltpu.roll(tiles[g], (32 + 32 * g) % 128, 1), spare)
        tiles = [jnp.where(lane8 < 96, tile, 0.0) for tile in tiles]
        return jnp.concatenate(tiles + [spare], axis=0)

    def field_rows(ref, i, count, inner):
        o = 1 if inner else 0
        return jnp.concatenate([ref[x + o, count * i + j + o] for j in range(count) for x in range(CX)], axis=1)

    for chunk in range(2):
        arrived(0, chunk)
        operate(0, chunk)
        send(1, chunk)

    def gram_zero(i, acc):
        v0 = field_rows(f1, i, GRAM, True)
        return acc + mm_nt(v0, v0)

    m0 = lax.fori_loop(0, CY // GRAM, gram_zero, jnp.zeros((NRHS, NRHS), F32))
    for chunk in range(2):
        arrived(1, chunk)
        operate(1, chunk)
        send(2, chunk)

    def gram_first(i, acc):
        v0, u1 = field_rows(f1, i, GRAM, True), field_rows(f2, i, GRAM, True)
        return acc + mm_nt(u1, jnp.concatenate([v0, u1], axis=0))

    first = lax.fori_loop(0, CY // GRAM, gram_first, jnp.zeros((NRHS, 64), F32))
    first = jnp.concatenate([m0, first, jnp.zeros((NRHS, 32), F32)], axis=1)
    lane32 = lanes((NRHS, 128))
    plane_send(first, plane_a, 0)

    arrived(2, 0)
    operate(2, 0)
    send(3, 0)
    line_send(plane_a, line_a, mid_a, 0)
    arrived(2, 1)
    operate(2, 1)
    send(3, 1)
    pair_send(line_a, pair_a, mid_a, 0)
    arrived(3, 0)
    operate(3, 0)
    sums = pair_take(pair_a, mid_a, 0)

    solved, inverse = eliminate([pltpu.roll(sums, 96, 1), sums])
    alpha0 = part(solved, 3)
    turn0 = mm(part(solved, 1), alpha0)
    eye = jnp.where(sublanes((NRHS, NRHS)) == lanes((NRHS, NRHS)), 1.0, 0.0)
    beta0 = turn0 - eye
    rho1 = mm(part(sums, 0), beta0)
    back0 = mm(part(inverse, 1), beta0)
    mix = jnp.concatenate([turn0, -alpha0], axis=0).T

    arrived(3, 1)
    operate(3, 1)

    def second_block(i, acc):
        v0, u1 = field_rows(f1, i, SECOND, True), field_rows(f2, i, SECOND, True)
        u2, u3 = field_rows(f3, i, SECOND, True), field_rows(f4, i, SECOND, False)
        top = jnp.concatenate([v0, u1, u2], axis=1)
        low = jnp.concatenate([u1, u2, u3], axis=1)
        new = mm(mix, jnp.concatenate([top, low], axis=0))
        n = 256 * SECOND
        p1, q1, aq1 = new[:, :n], new[:, n : 2 * n], new[:, 2 * n :]
        for j in range(SECOND):
            dirs[SECOND * i + j] = p1[:, 256 * j : 256 * j + 256]
            image[SECOND * i + j] = q1[:, 256 * j : 256 * j + 256]
        return acc + mm_nt(q1, jnp.concatenate([p1, q1, aq1], axis=0))

    grams = lax.fori_loop(0, CY // SECOND, second_block, jnp.zeros((NRHS, 96), F32))
    grams = jnp.concatenate([grams, jnp.zeros((NRHS, 32), F32)], axis=1)
    plane_send(grams, plane_b, 1)
    line_send(plane_b, line_b, mid_b, 1)
    pair_send(line_b, pair_b, mid_b, 1)
    sums = pair_take(pair_b, mid_b, 1)

    wide_rho = jnp.concatenate([rho1, jnp.zeros((NRHS, 96), F32)], axis=1)
    solved = eliminate([jnp.where(lane32 < 64, sums, pltpu.roll(wide_rho, 64, 1))])[0]
    alpha1 = part(solved, 2)
    turn1 = mm(part(solved, 1), alpha1)
    gram1, qq, qaq = part(sums, 0), part(sums, 1), part(sums, 2)
    gram2 = mm_t(alpha1, mm(qaq, alpha1) - mm(gram1, back0) - mm(qq, turn1))
    rho2 = mm(rho1, turn1 - eye)
    solved = eliminate([jnp.concatenate([gram2, rho2, jnp.zeros((NRHS, 64), F32)], axis=1)])[0]
    alpha2 = part(solved, 1)
    last = jnp.concatenate(
        [alpha0 - mm(beta0, alpha2), alpha1 + mm(turn1, alpha2), -mm(alpha1, alpha2)], axis=0
    ).T

    def finish(i, carry):
        old = [field_rows(f1, i, FINISH, True)]
        old += [jnp.concatenate([ref[FINISH * i + j] for j in range(FINISH)], axis=1) for ref in (dirs, image)]
        update = mm(last, jnp.concatenate(old, axis=0))
        for j in range(FINISH):
            for x in range(CX):
                piece = update[:, 128 * (2 * j + x) : 128 * (2 * j + x) + 128]
                value = f0[x + 1, FINISH * i + j + 1] + piece
                out_ref[pl.ds(CY * x + FINISH * i + j, NRHS, stride=CELLS), :] = value
        return carry

    lax.fori_loop(0, CY // FINISH, finish, 0)

    take(dummy.at[pl.ds(0, LABEL_TILES)], label_sem.at[0])
    for level in range(4):
        for chunk in range(2):
            take(dummy, halo_send.at[level, chunk])
    for index, (plane, line, pair) in enumerate(((plane_a, line_a, pair_a), (plane_b, line_b, pair_b))):
        take(plane.at[0:15], red_send.at[index, 0])
        take(line.at[0:7], red_send.at[index, 1])
        take(pair, red_send.at[index, 2])


def per_device(x_start, labels, conduct, electrodes):
    vmem = pl.BlockSpec(memory_space=pltpu.VMEM)
    field = pltpu.VMEM((CX + 2, CY + 2, NRHS, 128), F32)
    half = pltpu.VMEM((CY, NRHS, 256), F32)
    pack = pltpu.VMEM((2, 8, 128), F32)
    got = pltpu.VMEM((10, 2, 8, 128), F32)
    reduce = [
        pltpu.VMEM((16, 3, 8, 128), F32),
        pltpu.VMEM((8, 3, 8, 128), F32),
        pltpu.VMEM((3, 8, 128), F32),
        pltpu.VMEM((2, 3, 8, 128), F32),
        pltpu.VMEM((3, 8, 128), F32),
    ]
    out = pl.pallas_call(
        kernel,
        out_shape=jax.ShapeDtypeStruct((NRHS * CELLS, 128), F32),
        in_specs=[pl.BlockSpec(memory_space=pltpu.HBM)] * 4,
        out_specs=vmem,
        scratch_shapes=[
            pltpu.VMEM((NRHS * CELLS, 128), F32),
            pltpu.VMEM((CX, CY, 128), jnp.int32),
            pltpu.SMEM((LABELS, 9), F32),
            pltpu.SMEM((NRHS + 1,), jnp.int32),
            pltpu.SemaphoreType.DMA((4,)),
        ]
        + [field] * 4
        + [pltpu.VMEM((CX, CY, NRHS, 128), F32), half, half]
        + [
            pltpu.VMEM((18, CX, CY, 128), jnp.int32),
            pltpu.VMEM((3, CX + 2, 32, 128), jnp.int32),
            pltpu.VMEM((19, CELLS, 128), F32),
            pltpu.VMEM((19, CELLS, 8, 128), F32),
            pltpu.VMEM((5, 8, 128), F32),
        ]
        + [pack] * 4
        + [got] * 4
        + [pltpu.VMEM((2, 3, 8, 128), F32)]
        + reduce * 2
        + [
            pltpu.VMEM((HALO_TILES, 8, 128), F32),
            pltpu.SemaphoreType.DMA((4, 2)),
            pltpu.SemaphoreType.DMA((4, 2)),
            pltpu.SemaphoreType.DMA((2,)),
            pltpu.SemaphoreType.DMA((2, 3)),
            pltpu.SemaphoreType.DMA((2, 3)),
        ],
        compiler_params=pltpu.CompilerParams(
            collective_id=0, has_side_effects=True, vmem_limit_bytes=48 * 2**20
        ),
    )(x_start.reshape(NRHS * CELLS, 128), labels, conduct, electrodes)
    return out.reshape(x_start.shape)


def solution(mesh):
    return jax.shard_map(
        per_device,
        mesh=mesh,
        in_specs=(P(None, "gx", "gy", "gz"), P("gx", "gy", "gz"), P(), P()),
        out_specs=P(None, "gx", "gy", "gz"),
        check_vma=False,
    )
```

```python
import jax
import jax.numpy as jnp
from jax import lax
from jax.experimental import pallas as pl
from jax.experimental.pallas import tpu as pltpu
from jax.sharding import PartitionSpec as P

NRHS, LABELS = 32, 8
CX, CY, CZ = 2, 16, 128
GX, GY, GZ = 16, 4, 4
CELLS = CX * CY
F32 = jnp.float32
HIGH = lax.Precision.HIGHEST
MESH = pl.DeviceIdType.MESH

KINDS = {}
for kind, step in enumerate(
    ((1, 0, 0), (0, 1, 0), (0, 0, 1), (1, 1, 0), (1, -1, 0), (1, 0, 1), (1, 0, -1), (0, 1, 1), (0, 1, -1))
):
    KINDS[step] = kind
    KINDS[tuple(-s for s in step)] = kind
NEAR = sorted(KINDS)
CROSS = ((0, 0), (1, 0), (-1, 0), (0, 1), (0, -1))
FLAT = tuple(o for o in NEAR if o[2] == 0)
SIDE = tuple(o for o in NEAR if o[2] != 0)
PLANE = tuple((0, b, c) for b in range(GY) for c in range(GZ) if b or c)
LINE = tuple((2 * a, 0, 0) for a in range(1, GX // 2))
UNROLL = 8
GRAM = 8
SECOND = 8
FINISH = 8
HALO_TILES = 90
LABEL_TILES = 36


def wrapped(offset):
    return (offset[0] % GX, offset[1] % GY, offset[2] % GZ)


def coordinates():
    return lax.axis_index("gx"), lax.axis_index("gy"), lax.axis_index("gz")


def from_slot(offset, order):
    return order.index(tuple(-o for o in offset))


def mm(a, b):
    return jnp.dot(a, b, precision=HIGH, preferred_element_type=F32)


def mm_t(a, b):
    return lax.dot_general(a, b, (((0,), (0,)), ((), ())), precision=HIGH, preferred_element_type=F32)


def split(a):
    high = a.astype(jnp.bfloat16)
    return high, (a - high.astype(F32)).astype(jnp.bfloat16)


def mm_three(a, b):
    (a_high, a_low), (b_high, b_low) = split(a), split(b)
    total = jnp.dot(a_high, b_low, preferred_element_type=F32) + jnp.dot(a_low, b_high, preferred_element_type=F32)
    return total + jnp.dot(a_high, b_high, preferred_element_type=F32)


def mm_nt(a, b):
    return lax.dot_general(a, b, (((1,), (1,)), ((), ())), precision=HIGH, preferred_element_type=F32)


def lanes(shape):
    return lax.broadcasted_iota(jnp.int32, shape, 1)


def sublanes(shape):
    return lax.broadcasted_iota(jnp.int32, shape, 0)


def eliminate(matrices):
    sets = [[m[8 * g : 8 * g + 8] for g in range(4)] for m in matrices]
    row = sublanes((8, 128))
    width = 8
    for start in range(0, NRHS, width):
        panels = [
            [[jnp.broadcast_to(t[:, start + j : start + j + 1], (8, 128)) for t in tiles] for j in range(width)]
            for tiles in sets
        ]
        for j in range(width):
            own, inner = divmod(start + j, 8)
            for index, columns in enumerate(panels):
                scale = 1.0 / columns[j][own][inner : inner + 1]
                for which in [None] + list(range(j + 1, width)):
                    target = sets[index] if which is None else columns[which]
                    pivot = jnp.broadcast_to(target[own][inner : inner + 1] * scale, (8, 128))
                    new = [t - c * pivot for t, c in zip(target, columns[j])]
                    new[own] = jnp.where(row == inner, pivot, new[own])
                    if which is None:
                        sets[index] = new
                    else:
                        columns[which] = new
    return [jnp.concatenate(tiles, axis=0) for tiles in sets]


def part(matrix, index):
    if index:
        matrix = pltpu.roll(matrix, 128 - 32 * index, 1)
    return matrix[:, :NRHS]


def lookup(label, conduct, kind):
    value = jnp.zeros(label.shape, F32)
    for tissue in range(LABELS):
        value = jnp.where(label == tissue, conduct[tissue, kind], value)
    return value


def kernel(
    x_in, label_in, conduct_in, electrodes_in, out_ref,
    x_ref, label_ref, conduct, electrodes, in_sem,
    f0, f1, f2, f3, f4, dirs, image,
    label_got, padded, rows, weights, side_weights,
    pack0, pack1, pack2, pack3, got0, got1, got2, got3,
    give, plane_a, line_a, pair_a, mid_a, sum_a, plane_b, line_b, pair_b, mid_b, sum_b,
    dummy, halo_send, halo_recv, label_sem, red_send, red_recv,
):
    fields = (f0, f1, f2, f3)
    packs = (pack0, pack1, pack2, pack3)
    gots = (got0, got1, got2, got3)
    gx, gy, gz = coordinates()
    lane8 = lanes((8, 128))

    copies = [
        pltpu.make_async_copy(src, dst, in_sem.at[i])
        for i, (src, dst) in enumerate(
            ((x_in, x_ref), (label_in, label_ref), (conduct_in, conduct), (electrodes_in, electrodes))
        )
    ]
    for copy in copies:
        copy.start()

    partners = list(dict.fromkeys([wrapped(o) for o in NEAR] + list(PLANE) + list(LINE)))
    along = [
        {d: (c + d) & (n - 1) if d else c for d in sorted({p[a] for p in partners} | {0})}
        for a, (c, n) in enumerate(((gx, GX), (gy, GY), (gz, GZ)))
    ]

    def device(offset):
        return tuple(table[d] for table, d in zip(along, wrapped(offset)))

    barrier = pltpu.get_barrier_semaphore()
    for offset in partners:
        pl.semaphore_signal(barrier, inc=1, device_id=device(offset), device_id_type=MESH)

    copies[0].wait()
    for chunk in range(2):

        def load(i, acc, chunk=chunk):
            for inner in range(4):
                y = 4 * i + inner
                for x in range(CX):
                    tile = x_ref[pl.ds(512 * chunk + CY * x + y, 16, stride=CELLS), :]
                    f0[x + 1, y + 1, 16 * chunk : 16 * chunk + 16, :] = tile
                    for half in range(2):
                        spot = 32 * half + CY * x + y
                        moved = pltpu.roll(tile[8 * half : 8 * half + 8], 2 * spot + 1, 1)
                        acc = jnp.where(lane8 // 2 == spot, moved, acc)
            return acc

        pack0[chunk] = lax.fori_loop(0, CY // 4, load, jnp.zeros((8, 128), F32))
    for copy in copies[1:]:
        copy.wait()
    pl.semaphore_wait(barrier, len(partners))

    def put(src, dst, send, recv, offset):
        pltpu.make_async_remote_copy(
            src_ref=src, dst_ref=dst, send_sem=send, recv_sem=recv,
            device_id=device(offset), device_id_type=MESH,
        ).start()

    def take(ref, sem):
        pltpu.make_async_copy(ref, ref, sem).wait()

    def label_part(ref, offset):
        dx, dy, _ = offset
        xs = {0: pl.ds(0, CX), 1: pl.ds(CX - 1, 1), -1: pl.ds(0, 1)}[dx]
        ys = {0: pl.ds(0, CY), 1: pl.ds(CY - 8, 8), -1: pl.ds(0, 8)}[dy]
        return ref.at[xs, ys]

    x_from, x_to = {1: CX, -1: 1}, {1: 0, -1: CX + 1}
    y_from, y_to = {1: CY, -1: 1}, {1: 0, -1: CY + 1}

    def send_far(level, chunk):
        field, r = fields[level], pl.ds(16 * chunk, 16)
        ss, rs = halo_send.at[level, chunk], halo_recv.at[level, chunk]
        for dx in (1, -1):
            put(field.at[x_from[dx], 1 : CY + 1, r], field.at[x_to[dx], 1 : CY + 1, r], ss, rs, (dx, 0, 0))

    def send_near(level, chunk):
        field, pack, got = fields[level], packs[level], gots[level]
        r = pl.ds(16 * chunk, 16)
        ss, rs = halo_send.at[level, chunk], halo_recv.at[level, chunk]
        for slot, offset in enumerate(SIDE):
            put(pack.at[chunk], got.at[slot, chunk], ss, rs, offset)
        for dy in (1, -1):
            put(field.at[1 : CX + 1, y_from[dy], r], field.at[1 : CX + 1, y_to[dy], r], ss, rs, (0, dy, 0))
        for dx in (1, -1):
            for dy in (1, -1):
                put(field.at[x_from[dx], y_from[dy], r], field.at[x_to[dx], y_to[dy], r], ss, rs, (dx, dy, 0))

    def send(level, chunk):
        send_far(level, chunk)
        send_near(level, chunk)

    for slot, offset in enumerate(NEAR):
        put(label_part(label_ref, offset), label_part(label_got.at[slot], offset), label_sem.at[0], label_sem.at[1], offset)
    send_far(0, 0)
    send_near(0, 0)
    send(0, 1)

    owns = [[lookup(label_ref[x], conduct, kind) for kind in range(9)] for x in range(CX)]
    take(dummy.at[pl.ds(0, LABEL_TILES)], label_sem.at[1])
    inside = {
        (0, 1): gx < GX - 1, (0, -1): gx > 0, (1, 1): gy < GY - 1, (1, -1): gy > 0, (2, 1): gz < GZ - 1, (2, -1): gz > 0,
    }

    def block(offset, x, top):
        ref = label_ref if offset == (0, 0, 0) else label_got.at[from_slot(offset, NEAR)]
        if top is None:
            return ref[x]
        return ref[x, CY - 8 : CY] if top < 0 else ref[x, 0:8]

    def put_rows(shift, xx, dx, dy):
        x = {0: xx - 1, 1: 0, -1: CX - 1}[dx]
        value = block((dx, dy, 0), x, dy or None)
        lane = lanes(value.shape)
        if shift:
            other = block((dx, dy, shift), x, dy or None)
            other = jnp.where(inside[2, shift], other, -1)
            edge = 127 if shift == 1 else 0
            value = jnp.where(lane == edge, pltpu.roll(other, (-shift) % 128, 1), pltpu.roll(value, (-shift) % 128, 1))
        if dx:
            value = jnp.where(inside[0, dx], value, -1)
        if dy:
            value = jnp.where(inside[1, dy], value, -1)
        row = {0: 8, 1: 24, -1: 0}[dy]
        padded[shift + 1, xx, row : row + value.shape[0], :] = value

    for shift in (0, 1, -1):
        for xx in range(CX + 2):
            dx = -1 if xx == 0 else (1 if xx == CX + 1 else 0)
            put_rows(shift, xx, dx, 0)
            if dx == 0 or shift == 0:
                put_rows(shift, xx, dx, 1)
                put_rows(shift, xx, dx, -1)

    for x in range(CX):
        own = owns[x]
        total = jnp.zeros((CY, 128), F32)
        for offset in NEAR:
            dx, dy, dz = offset
            there = padded[dz + 1, x + 1 + dx, 8 + dy : 24 + dy, :]
            kind = KINDS[offset]
            weight = 0.5 * (own[kind] + lookup(there, conduct, kind))
            total = total + weight
            weight = jnp.where(there >= 0, weight, 0.0)
            if dz:
                weight = pltpu.roll(weight, dz % 128, 1)
                index = 9 + 5 * (dz < 0) + CROSS.index((dx, dy))
            else:
                index = 1 + FLAT.index(offset)
            rows[index, CY * x : CY * x + CY, :] = weight
        rows[0, CY * x : CY * x + CY, :] = total

    def spread(c, carry):
        for index in range(19):
            weights[index, c] = jnp.broadcast_to(rows[index, pl.ds(c, 1), :], (8, 128))
        return carry

    lax.fori_loop(0, CELLS, spread, 0)

    pair_lane = lanes((CELLS, 128))
    keep = (pair_lane % 64) // 2 == sublanes((CELLS, 128))
    for f in range(5):
        up = jnp.broadcast_to(rows[9 + f][:, 0:1], (CELLS, 128))
        down = jnp.broadcast_to(rows[14 + f][:, 127:128], (CELLS, 128))
        both = jnp.where(keep, jnp.where(pair_lane % 2 == 1, up, down), 0.0)
        side_weights[f] = jnp.broadcast_to(jnp.sum(both, axis=0, keepdims=True), (8, 128))

    flat_base = gx * (CX * GY * CY * GZ * CZ) + gy * (CY * GZ * CZ) + gz * CZ
    row8 = sublanes((8, 128))
    wanted = []
    for g in range(4):
        tile = jnp.zeros((8, 128), jnp.int32)
        for i in range(8):
            tile = jnp.where(row8 == i, electrodes[8 * g + i], tile)
        wanted.append(tile)
    common = electrodes[NRHS]

    def operate(level, chunk):
        src, got, base = fields[level], gots[level], 16 * chunk
        dst = f4 if level == 3 else fields[level + 1]

        def sides(dx, dy):
            up = got[from_slot((dx, dy, 1), SIDE), chunk]
            down = got[from_slot((dx, dy, -1), SIDE), chunk]
            return jnp.where(lane8 % 2 == 1, up, down)

        center = sides(0, 0)
        cell_x, cell_y = (lane8 % 64) // 32, (lane8 % 32) // 2
        parts = {
            (0, 0): center,
            (1, 0): jnp.where(cell_x == 1, pltpu.roll(sides(1, 0), 32, 1), pltpu.roll(center, 96, 1)),
            (-1, 0): jnp.where(cell_x == 0, pltpu.roll(sides(-1, 0), 96, 1), pltpu.roll(center, 32, 1)),
            (0, 1): jnp.where(cell_y == 15, pltpu.roll(sides(0, 1), 30, 1), pltpu.roll(center, 126, 1)),
            (0, -1): jnp.where(cell_y == 0, pltpu.roll(sides(0, -1), 98, 1), pltpu.roll(center, 2, 1)),
        }
        end = jnp.zeros((8, 128), F32)
        for f, cross in enumerate(CROSS):
            end = end + side_weights[f] * parts[cross]

        def body(i, acc):
            held, loaded, results = {}, {}, []

            def weight(index, c, key):
                if (index, key) not in held:
                    held[index, key] = weights[index, c]
                return held[index, key]

            def field(xx, inner, half):
                if (xx, inner, half) not in loaded:
                    loaded[xx, inner, half] = src[xx, UNROLL * i + inner, pl.ds(base + 8 * half, 8), :]
                return loaded[xx, inner, half]

            for inner in range(UNROLL):
                y = UNROLL * i + inner
                for x in range(CX):
                    c = CY * x + y
                    for half in range(2):
                        key = (x, inner)
                        u = {
                            (dx, dy): field(x + 1 + dx, inner + 1 + dy, half) for dx in (-1, 0, 1) for dy in (-1, 0, 1)
                        }
                        value = weight(0, c, key) * u[0, 0]
                        for k, offset in enumerate(FLAT):
                            value = value - weight(1 + k, c, key) * u[offset[0], offset[1]]
                        up = weight(9, c, key) * u[0, 0]
                        down = weight(14, c, key) * u[0, 0]
                        for f in range(1, 5):
                            up = up + weight(9 + f, c, key) * u[CROSS[f]]
                            down = down + weight(14 + f, c, key) * u[CROSS[f]]
                        spot = 32 * half + c
                        side = pltpu.roll(end, 127 - 2 * spot, 1)
                        up = jnp.where(lane8 == 0, side, up)
                        down = jnp.where(lane8 == 127, side, down)
                        value = value - pltpu.roll(up, 127, 1) - pltpu.roll(down, 1, 1)
                        if level == 0:
                            flat = flat_base + x * (GY * CY * GZ * CZ) + y * (GZ * CZ) + lane8
                            hit = jnp.where(flat == wanted[2 * chunk + half], 40.0, 0.0)
                            value = (hit - jnp.where(flat == common, 40.0, 0.0)) - value
                        if level < 3:
                            acc = jnp.where(lane8 // 2 == spot, pltpu.roll(value, 2 * spot + 1, 1), acc)
                        results.append((x, y, half, value))
            for x, y, half, value in results:
                if level == 3:
                    dst[x, y, pl.ds(base + 8 * half, 8), :] = value
                else:
                    dst[x + 1, y + 1, pl.ds(base + 8 * half, 8), :] = value
            return acc

        acc = lax.fori_loop(0, CY // UNROLL, body, jnp.zeros((8, 128), F32))
        if level < 3:
            packs[level + 1][chunk] = acc

    def arrived(level, chunk):
        take(dummy, halo_recv.at[level, chunk])

    mine = gy * GZ + gz
    chip = gx // 2

    def plane_send(value, got, index):
        spare = value[24:32]
        for g in range(3):
            tile = jnp.where(lane8 < 96, value[8 * g : 8 * g + 8], pltpu.roll(spare, 96 - 32 * g, 1))
            give[index, g] = tile
            got[mine, g] = tile
        for offset in PLANE:
            put(give.at[index], got.at[mine], red_send.at[index, 0], red_recv.at[index, 0], offset)

    def line_send(plane, got, mid, index):
        take(plane.at[0:15], red_recv.at[index, 0])
        value = plane[0]
        for i in range(1, 16):
            value = value + plane[i]
        mid[0] = value
        got[chip] = value
        for offset in LINE:
            put(mid.at[0], got.at[chip], red_send.at[index, 1], red_recv.at[index, 1], offset)

    def pair_send(line, got, mid, index):
        take(line.at[0:7], red_recv.at[index, 1])
        value = line[0]
        for i in range(1, 8):
            value = value + line[i]
        mid[1] = value
        pltpu.make_async_remote_copy(
            src_ref=mid.at[1], dst_ref=got, send_sem=red_send.at[index, 2], recv_sem=red_recv.at[index, 2],
            device_id=(gx + 1 - 2 * lax.rem(gx, 2), gy, gz), device_id_type=MESH,
        ).start()

    def pair_take(got, mid, index):
        take(got, red_recv.at[index, 2])
        tiles = [mid[1, g] + got[g] for g in range(3)]
        spare = jnp.zeros((8, 128), F32)
        for g in range(3):
            spare = jnp.where(lane8 // 32 == g, pltpu.roll(tiles[g], (32 + 32 * g) % 128, 1), spare)
        tiles = [jnp.where(lane8 < 96, tile, 0.0) for tile in tiles]
        return jnp.concatenate(tiles + [spare], axis=0)

    def field_rows(ref, i, count, inner):
        o = 1 if inner else 0
        return jnp.concatenate([ref[x + o, count * i + j + o] for j in range(count) for x in range(CX)], axis=1)

    for chunk in range(2):
        arrived(0, chunk)
        operate(0, chunk)
        send(1, chunk)

    def gram_zero(i, acc):
        v0 = field_rows(f1, i, GRAM, True)
        return acc + mm_nt(v0, v0)

    m0 = lax.fori_loop(0, CY // GRAM, gram_zero, jnp.zeros((NRHS, NRHS), F32))
    for chunk in range(2):
        arrived(1, chunk)
        operate(1, chunk)
        send(2, chunk)

    def gram_first(i, acc):
        v0, u1 = field_rows(f1, i, GRAM, True), field_rows(f2, i, GRAM, True)
        return acc + mm_nt(u1, jnp.concatenate([v0, u1], axis=0))

    first = lax.fori_loop(0, CY // GRAM, gram_first, jnp.zeros((NRHS, 64), F32))
    first = jnp.concatenate([m0, first, jnp.zeros((NRHS, 32), F32)], axis=1)
    lane32 = lanes((NRHS, 128))
    plane_send(first, plane_a, 0)

    for chunk in range(2):
        arrived(2, chunk)
        operate(2, chunk)
        send(3, chunk)
    line_send(plane_a, line_a, mid_a, 0)
    for chunk in range(2):
        arrived(3, chunk)
        operate(3, chunk)
    pair_send(line_a, pair_a, mid_a, 0)
    sums = pair_take(pair_a, mid_a, 0)

    solved, inverse = eliminate([pltpu.roll(sums, 96, 1), sums])
    alpha0 = part(solved, 3)
    turn0 = mm(part(solved, 1), alpha0)
    eye = jnp.where(sublanes((NRHS, NRHS)) == lanes((NRHS, NRHS)), 1.0, 0.0)
    beta0 = turn0 - eye
    rho1 = mm(part(sums, 0), beta0)
    back0 = mm(part(inverse, 1), beta0)
    mix = jnp.concatenate([turn0, -alpha0], axis=0).T

    def second_block(i, acc):
        v0, u1 = field_rows(f1, i, SECOND, True), field_rows(f2, i, SECOND, True)
        u2, u3 = field_rows(f3, i, SECOND, True), field_rows(f4, i, SECOND, False)
        top = jnp.concatenate([v0, u1, u2], axis=1)
        low = jnp.concatenate([u1, u2, u3], axis=1)
        new = mm(mix, jnp.concatenate([top, low], axis=0))
        n = 256 * SECOND
        p1, q1, aq1 = new[:, :n], new[:, n : 2 * n], new[:, 2 * n :]
        for j in range(SECOND):
            dirs[SECOND * i + j] = p1[:, 256 * j : 256 * j + 256]
            image[SECOND * i + j] = q1[:, 256 * j : 256 * j + 256]
        return acc + mm_nt(q1, jnp.concatenate([p1, q1, aq1], axis=0))

    grams = lax.fori_loop(0, CY // SECOND, second_block, jnp.zeros((NRHS, 96), F32))
    grams = jnp.concatenate([grams, jnp.zeros((NRHS, 32), F32)], axis=1)
    plane_send(grams, plane_b, 1)
    line_send(plane_b, line_b, mid_b, 1)
    pair_send(line_b, pair_b, mid_b, 1)
    sums = pair_take(pair_b, mid_b, 1)

    wide_rho = jnp.concatenate([rho1, jnp.zeros((NRHS, 96), F32)], axis=1)
    solved = eliminate([jnp.where(lane32 < 64, sums, pltpu.roll(wide_rho, 64, 1))])[0]
    alpha1 = part(solved, 2)
    turn1 = mm(part(solved, 1), alpha1)
    gram1, qq, qaq = part(sums, 0), part(sums, 1), part(sums, 2)
    gram2 = mm_t(alpha1, mm(qaq, alpha1) - mm(gram1, back0) - mm(qq, turn1))
    rho2 = mm(rho1, turn1 - eye)
    solved = eliminate([jnp.concatenate([gram2, rho2, jnp.zeros((NRHS, 64), F32)], axis=1)])[0]
    alpha2 = part(solved, 1)
    last = jnp.concatenate(
        [alpha0 - mm(beta0, alpha2), alpha1 + mm(turn1, alpha2), -mm(alpha1, alpha2)], axis=0
    ).T

    def finish(i, carry):
        old = [field_rows(f1, i, FINISH, True)]
        old += [jnp.concatenate([ref[FINISH * i + j] for j in range(FINISH)], axis=1) for ref in (dirs, image)]
        update = mm_three(last, jnp.concatenate(old, axis=0))
        for j in range(FINISH):
            for x in range(CX):
                piece = update[:, 128 * (2 * j + x) : 128 * (2 * j + x) + 128]
                value = f0[x + 1, FINISH * i + j + 1] + piece
                out_ref[pl.ds(CY * x + FINISH * i + j, NRHS, stride=CELLS), :] = value
        return carry

    lax.fori_loop(0, CY // FINISH, finish, 0)

    take(dummy.at[pl.ds(0, LABEL_TILES)], label_sem.at[0])
    for level in range(4):
        for chunk in range(2):
            take(dummy, halo_send.at[level, chunk])
    for index, (plane, line, pair) in enumerate(((plane_a, line_a, pair_a), (plane_b, line_b, pair_b))):
        take(plane.at[0:15], red_send.at[index, 0])
        take(line.at[0:7], red_send.at[index, 1])
        take(pair, red_send.at[index, 2])


def per_device(x_start, labels, conduct, electrodes):
    vmem = pl.BlockSpec(memory_space=pltpu.VMEM)
    field = pltpu.VMEM((CX + 2, CY + 2, NRHS, 128), F32)
    half = pltpu.VMEM((CY, NRHS, 256), F32)
    pack = pltpu.VMEM((2, 8, 128), F32)
    got = pltpu.VMEM((10, 2, 8, 128), F32)
    reduce = [
        pltpu.VMEM((16, 3, 8, 128), F32),
        pltpu.VMEM((8, 3, 8, 128), F32),
        pltpu.VMEM((3, 8, 128), F32),
        pltpu.VMEM((2, 3, 8, 128), F32),
        pltpu.VMEM((3, 8, 128), F32),
    ]
    out = pl.pallas_call(
        kernel,
        out_shape=jax.ShapeDtypeStruct((NRHS * CELLS, 128), F32),
        in_specs=[pl.BlockSpec(memory_space=pltpu.HBM)] * 4,
        out_specs=vmem,
        scratch_shapes=[
            pltpu.VMEM((NRHS * CELLS, 128), F32),
            pltpu.VMEM((CX, CY, 128), jnp.int32),
            pltpu.SMEM((LABELS, 9), F32),
            pltpu.SMEM((NRHS + 1,), jnp.int32),
            pltpu.SemaphoreType.DMA((4,)),
        ]
        + [field] * 4
        + [pltpu.VMEM((CX, CY, NRHS, 128), F32), half, half]
        + [
            pltpu.VMEM((18, CX, CY, 128), jnp.int32),
            pltpu.VMEM((3, CX + 2, 32, 128), jnp.int32),
            pltpu.VMEM((19, CELLS, 128), F32),
            pltpu.VMEM((19, CELLS, 8, 128), F32),
            pltpu.VMEM((5, 8, 128), F32),
        ]
        + [pack] * 4
        + [got] * 4
        + [pltpu.VMEM((2, 3, 8, 128), F32)]
        + reduce * 2
        + [
            pltpu.VMEM((HALO_TILES, 8, 128), F32),
            pltpu.SemaphoreType.DMA((4, 2)),
            pltpu.SemaphoreType.DMA((4, 2)),
            pltpu.SemaphoreType.DMA((2,)),
            pltpu.SemaphoreType.DMA((2, 3)),
            pltpu.SemaphoreType.DMA((2, 3)),
        ],
        compiler_params=pltpu.CompilerParams(
            collective_id=0, has_side_effects=True, vmem_limit_bytes=48 * 2**20
        ),
    )(x_start.reshape(NRHS * CELLS, 128), labels, conduct, electrodes)
    return out.reshape(x_start.shape)


def solution(mesh):
    return jax.shard_map(
        per_device,
        mesh=mesh,
        in_specs=(P(None, "gx", "gy", "gz"), P("gx", "gy", "gz"), P(), P()),
        out_specs=P(None, "gx", "gy", "gz"),
        check_vma=False,
    )
```

```python
import jax
import jax.numpy as jnp
from jax import lax
from jax.experimental import pallas as pl
from jax.experimental.pallas import tpu as pltpu
from jax.sharding import PartitionSpec as P

NRHS, LABELS = 32, 8
CX, CY, CZ = 2, 16, 128
GX, GY, GZ = 16, 4, 4
CELLS = CX * CY
F32 = jnp.float32
HIGH = lax.Precision.HIGHEST
MESH = pl.DeviceIdType.MESH

KINDS = {}
for kind, step in enumerate(
    ((1, 0, 0), (0, 1, 0), (0, 0, 1), (1, 1, 0), (1, -1, 0), (1, 0, 1), (1, 0, -1), (0, 1, 1), (0, 1, -1))
):
    KINDS[step] = kind
    KINDS[tuple(-s for s in step)] = kind
NEAR = sorted(KINDS)
CROSS = ((0, 0), (1, 0), (-1, 0), (0, 1), (0, -1))
FLAT = tuple(o for o in NEAR if o[2] == 0)
SIDE = tuple(o for o in NEAR if o[2] != 0)
PLANE = tuple((0, b, c) for b in range(GY) for c in range(GZ) if b or c)
LINE = tuple((2 * a, 0, 0) for a in range(1, GX // 2))
UNROLL = 8
GRAM = 8
SECOND = 8
FINISH = 8
HALO_TILES = 90
LABEL_TILES = 36


def wrapped(offset):
    return (offset[0] % GX, offset[1] % GY, offset[2] % GZ)


def coordinates():
    return lax.axis_index("gx"), lax.axis_index("gy"), lax.axis_index("gz")


def from_slot(offset, order):
    return order.index(tuple(-o for o in offset))


def mm(a, b):
    return jnp.dot(a, b, precision=HIGH, preferred_element_type=F32)


def mm_t(a, b):
    return lax.dot_general(a, b, (((0,), (0,)), ((), ())), precision=HIGH, preferred_element_type=F32)


def split(a):
    high = a.astype(jnp.bfloat16)
    return high, (a - high.astype(F32)).astype(jnp.bfloat16)


def mm_three(a, b):
    (a_high, a_low), (b_high, b_low) = split(a), split(b)
    total = jnp.dot(a_high, b_low, preferred_element_type=F32) + jnp.dot(a_low, b_high, preferred_element_type=F32)
    return total + jnp.dot(a_high, b_high, preferred_element_type=F32)


def mm_nt(a, b):
    return lax.dot_general(a, b, (((1,), (1,)), ((), ())), precision=HIGH, preferred_element_type=F32)


def lanes(shape):
    return lax.broadcasted_iota(jnp.int32, shape, 1)


def sublanes(shape):
    return lax.broadcasted_iota(jnp.int32, shape, 0)


def eliminate(matrices):
    sets = [[m[8 * g : 8 * g + 8] for g in range(4)] for m in matrices]
    row = sublanes((8, 128))
    width = 16
    for start in range(0, NRHS, width):
        panels = [
            [[jnp.broadcast_to(t[:, start + j : start + j + 1], (8, 128)) for t in tiles] for j in range(width)]
            for tiles in sets
        ]
        for j in range(width):
            own, inner = divmod(start + j, 8)
            for index, columns in enumerate(panels):
                scale = 1.0 / columns[j][own][inner : inner + 1]
                for which in [None] + list(range(j + 1, width)):
                    target = sets[index] if which is None else columns[which]
                    pivot = jnp.broadcast_to(target[own][inner : inner + 1] * scale, (8, 128))
                    new = [t - c * pivot for t, c in zip(target, columns[j])]
                    new[own] = jnp.where(row == inner, pivot, new[own])
                    if which is None:
                        sets[index] = new
                    else:
                        columns[which] = new
    return [jnp.concatenate(tiles, axis=0) for tiles in sets]


def part(matrix, index):
    if index:
        matrix = pltpu.roll(matrix, 128 - 32 * index, 1)
    return matrix[:, :NRHS]


def lookup(label, conduct, kind):
    value = jnp.zeros(label.shape, F32)
    for tissue in range(LABELS):
        value = jnp.where(label == tissue, conduct[tissue, kind], value)
    return value


def kernel(
    x_in, label_in, conduct_in, electrodes_in, out_ref,
    x_ref, label_ref, conduct, electrodes, in_sem,
    f0, f1, f2, f3, f4, dirs, image,
    label_got, padded, rows, weights, side_weights,
    pack0, pack1, pack2, pack3, got0, got1, got2, got3,
    give, plane_a, line_a, pair_a, mid_a, sum_a, plane_b, line_b, pair_b, mid_b, sum_b,
    dummy, halo_send, halo_recv, label_sem, red_send, red_recv,
):
    fields = (f0, f1, f2, f3)
    packs = (pack0, pack1, pack2, pack3)
    gots = (got0, got1, got2, got3)
    gx, gy, gz = coordinates()
    lane8 = lanes((8, 128))

    copies = [
        pltpu.make_async_copy(src, dst, in_sem.at[i])
        for i, (src, dst) in enumerate(
            ((x_in, x_ref), (label_in, label_ref), (conduct_in, conduct), (electrodes_in, electrodes))
        )
    ]
    for copy in copies:
        copy.start()

    partners = list(dict.fromkeys([wrapped(o) for o in NEAR] + list(PLANE) + list(LINE)))
    along = [
        {d: (c + d) & (n - 1) if d else c for d in sorted({p[a] for p in partners} | {0})}
        for a, (c, n) in enumerate(((gx, GX), (gy, GY), (gz, GZ)))
    ]

    def device(offset):
        return tuple(table[d] for table, d in zip(along, wrapped(offset)))

    barrier = pltpu.get_barrier_semaphore()
    for offset in partners:
        pl.semaphore_signal(barrier, inc=1, device_id=device(offset), device_id_type=MESH)

    copies[0].wait()
    for chunk in range(2):

        def load(i, acc, chunk=chunk):
            for inner in range(4):
                y = 4 * i + inner
                for x in range(CX):
                    tile = x_ref[pl.ds(512 * chunk + CY * x + y, 16, stride=CELLS), :]
                    f0[x + 1, y + 1, 16 * chunk : 16 * chunk + 16, :] = tile
                    for half in range(2):
                        spot = 32 * half + CY * x + y
                        moved = pltpu.roll(tile[8 * half : 8 * half + 8], 2 * spot + 1, 1)
                        acc = jnp.where(lane8 // 2 == spot, moved, acc)
            return acc

        pack0[chunk] = lax.fori_loop(0, CY // 4, load, jnp.zeros((8, 128), F32))
    for copy in copies[1:]:
        copy.wait()
    pl.semaphore_wait(barrier, len(partners))

    def put(src, dst, send, recv, offset):
        pltpu.make_async_remote_copy(
            src_ref=src, dst_ref=dst, send_sem=send, recv_sem=recv,
            device_id=device(offset), device_id_type=MESH,
        ).start()

    def take(ref, sem):
        pltpu.make_async_copy(ref, ref, sem).wait()

    def label_part(ref, offset):
        dx, dy, _ = offset
        xs = {0: pl.ds(0, CX), 1: pl.ds(CX - 1, 1), -1: pl.ds(0, 1)}[dx]
        ys = {0: pl.ds(0, CY), 1: pl.ds(CY - 8, 8), -1: pl.ds(0, 8)}[dy]
        return ref.at[xs, ys]

    x_from, x_to = {1: CX, -1: 1}, {1: 0, -1: CX + 1}
    y_from, y_to = {1: CY, -1: 1}, {1: 0, -1: CY + 1}

    def send_far(level, chunk, ys=slice(1, CY + 1)):
        field, r = fields[level], pl.ds(16 * chunk, 16)
        ss, rs = halo_send.at[level, chunk], halo_recv.at[level, chunk]
        for dx in (1, -1):
            put(field.at[x_from[dx], ys, r], field.at[x_to[dx], ys, r], ss, rs, (dx, 0, 0))

    def send_near(level, chunk):
        field, pack, got = fields[level], packs[level], gots[level]
        r = pl.ds(16 * chunk, 16)
        ss, rs = halo_send.at[level, chunk], halo_recv.at[level, chunk]
        for slot, offset in enumerate(SIDE):
            put(pack.at[chunk], got.at[slot, chunk], ss, rs, offset)
        for dy in (1, -1):
            put(field.at[1 : CX + 1, y_from[dy], r], field.at[1 : CX + 1, y_to[dy], r], ss, rs, (0, dy, 0))
        for dx in (1, -1):
            for dy in (1, -1):
                put(field.at[x_from[dx], y_from[dy], r], field.at[x_to[dx], y_to[dy], r], ss, rs, (dx, dy, 0))

    def send(level, chunk):
        send_far(level, chunk)
        send_near(level, chunk)

    for slot, offset in enumerate(NEAR):
        put(label_part(label_ref, offset), label_part(label_got.at[slot], offset), label_sem.at[0], label_sem.at[1], offset)
    send_far(0, 0)
    send_near(0, 0)
    send(0, 1)

    owns = [[lookup(label_ref[x], conduct, kind) for kind in range(9)] for x in range(CX)]
    take(dummy.at[pl.ds(0, LABEL_TILES)], label_sem.at[1])
    inside = {
        (0, 1): gx < GX - 1, (0, -1): gx > 0, (1, 1): gy < GY - 1, (1, -1): gy > 0, (2, 1): gz < GZ - 1, (2, -1): gz > 0,
    }

    def block(offset, x, top):
        ref = label_ref if offset == (0, 0, 0) else label_got.at[from_slot(offset, NEAR)]
        if top is None:
            return ref[x]
        return ref[x, CY - 8 : CY] if top < 0 else ref[x, 0:8]

    def put_rows(shift, xx, dx, dy):
        x = {0: xx - 1, 1: 0, -1: CX - 1}[dx]
        value = block((dx, dy, 0), x, dy or None)
        lane = lanes(value.shape)
        if shift:
            other = block((dx, dy, shift), x, dy or None)
            other = jnp.where(inside[2, shift], other, -1)
            edge = 127 if shift == 1 else 0
            value = jnp.where(lane == edge, pltpu.roll(other, (-shift) % 128, 1), pltpu.roll(value, (-shift) % 128, 1))
        if dx:
            value = jnp.where(inside[0, dx], value, -1)
        if dy:
            value = jnp.where(inside[1, dy], value, -1)
        row = {0: 8, 1: 24, -1: 0}[dy]
        padded[shift + 1, xx, row : row + value.shape[0], :] = value

    for shift in (0, 1, -1):
        for xx in range(CX + 2):
            dx = -1 if xx == 0 else (1 if xx == CX + 1 else 0)
            put_rows(shift, xx, dx, 0)
            if dx == 0 or shift == 0:
                put_rows(shift, xx, dx, 1)
                put_rows(shift, xx, dx, -1)

    for x in range(CX):
        own = owns[x]
        total = jnp.zeros((CY, 128), F32)
        for offset in NEAR:
            dx, dy, dz = offset
            there = padded[dz + 1, x + 1 + dx, 8 + dy : 24 + dy, :]
            kind = KINDS[offset]
            weight = 0.5 * (own[kind] + lookup(there, conduct, kind))
            total = total + weight
            weight = jnp.where(there >= 0, weight, 0.0)
            if dz:
                weight = pltpu.roll(weight, dz % 128, 1)
                index = 9 + 5 * (dz < 0) + CROSS.index((dx, dy))
            else:
                index = 1 + FLAT.index(offset)
            rows[index, CY * x : CY * x + CY, :] = weight
        rows[0, CY * x : CY * x + CY, :] = total

    def spread(c, carry):
        for index in range(19):
            weights[index, c] = jnp.broadcast_to(rows[index, pl.ds(c, 1), :], (8, 128))
        return carry

    lax.fori_loop(0, CELLS, spread, 0)

    pair_lane = lanes((CELLS, 128))
    keep = (pair_lane % 64) // 2 == sublanes((CELLS, 128))
    for f in range(5):
        up = jnp.broadcast_to(rows[9 + f][:, 0:1], (CELLS, 128))
        down = jnp.broadcast_to(rows[14 + f][:, 127:128], (CELLS, 128))
        both = jnp.where(keep, jnp.where(pair_lane % 2 == 1, up, down), 0.0)
        side_weights[f] = jnp.broadcast_to(jnp.sum(both, axis=0, keepdims=True), (8, 128))

    flat_base = gx * (CX * GY * CY * GZ * CZ) + gy * (CY * GZ * CZ) + gz * CZ
    row8 = sublanes((8, 128))
    wanted = []
    for g in range(4):
        tile = jnp.zeros((8, 128), jnp.int32)
        for i in range(8):
            tile = jnp.where(row8 == i, electrodes[8 * g + i], tile)
        wanted.append(tile)
    common = electrodes[NRHS]

    def operate(level, chunk):
        src, got, base = fields[level], gots[level], 16 * chunk
        dst = f4 if level == 3 else fields[level + 1]

        def sides(dx, dy):
            up = got[from_slot((dx, dy, 1), SIDE), chunk]
            down = got[from_slot((dx, dy, -1), SIDE), chunk]
            return jnp.where(lane8 % 2 == 1, up, down)

        center = sides(0, 0)
        cell_x, cell_y = (lane8 % 64) // 32, (lane8 % 32) // 2
        parts = {
            (0, 0): center,
            (1, 0): jnp.where(cell_x == 1, pltpu.roll(sides(1, 0), 32, 1), pltpu.roll(center, 96, 1)),
            (-1, 0): jnp.where(cell_x == 0, pltpu.roll(sides(-1, 0), 96, 1), pltpu.roll(center, 32, 1)),
            (0, 1): jnp.where(cell_y == 15, pltpu.roll(sides(0, 1), 30, 1), pltpu.roll(center, 126, 1)),
            (0, -1): jnp.where(cell_y == 0, pltpu.roll(sides(0, -1), 98, 1), pltpu.roll(center, 2, 1)),
        }
        end = jnp.zeros((8, 128), F32)
        for f, cross in enumerate(CROSS):
            end = end + side_weights[f] * parts[cross]

        def body(i, acc):
            held, loaded, results = {}, {}, []

            def weight(index, c, key):
                if (index, key) not in held:
                    held[index, key] = weights[index, c]
                return held[index, key]

            def field(xx, inner, half):
                if (xx, inner, half) not in loaded:
                    loaded[xx, inner, half] = src[xx, UNROLL * i + inner, pl.ds(base + 8 * half, 8), :]
                return loaded[xx, inner, half]

            for inner in range(UNROLL):
                y = UNROLL * i + inner
                for x in range(CX):
                    c = CY * x + y
                    for half in range(2):
                        key = (x, inner)
                        u = {
                            (dx, dy): field(x + 1 + dx, inner + 1 + dy, half) for dx in (-1, 0, 1) for dy in (-1, 0, 1)
                        }
                        value = weight(0, c, key) * u[0, 0]
                        for k, offset in enumerate(FLAT):
                            value = value - weight(1 + k, c, key) * u[offset[0], offset[1]]
                        up = weight(9, c, key) * u[0, 0]
                        down = weight(14, c, key) * u[0, 0]
                        for f in range(1, 5):
                            up = up + weight(9 + f, c, key) * u[CROSS[f]]
                            down = down + weight(14 + f, c, key) * u[CROSS[f]]
                        spot = 32 * half + c
                        side = pltpu.roll(end, 127 - 2 * spot, 1)
                        up = jnp.where(lane8 == 0, side, up)
                        down = jnp.where(lane8 == 127, side, down)
                        value = value - pltpu.roll(up, 127, 1) - pltpu.roll(down, 1, 1)
                        if level == 0:
                            flat = flat_base + x * (GY * CY * GZ * CZ) + y * (GZ * CZ) + lane8
                            hit = jnp.where(flat == wanted[2 * chunk + half], 40.0, 0.0)
                            value = (hit - jnp.where(flat == common, 40.0, 0.0)) - value
                        if level < 3:
                            acc = jnp.where(lane8 // 2 == spot, pltpu.roll(value, 2 * spot + 1, 1), acc)
                        results.append((x, y, half, value))
            for x, y, half, value in results:
                if level == 3:
                    dst[x, y, pl.ds(base + 8 * half, 8), :] = value
                else:
                    dst[x + 1, y + 1, pl.ds(base + 8 * half, 8), :] = value
            return acc

        acc = jnp.zeros((8, 128), F32)
        for i in range(CY // UNROLL):
            acc = body(i, acc)
            if level < 3:
                send_far(level + 1, chunk, slice(UNROLL * i + 1, UNROLL * (i + 1) + 1))
        if level < 3:
            packs[level + 1][chunk] = acc

    def arrived(level, chunk):
        take(dummy, halo_recv.at[level, chunk])

    mine = gy * GZ + gz
    chip = gx // 2

    def plane_send(value, got, index):
        spare = value[24:32]
        for g in range(3):
            tile = jnp.where(lane8 < 96, value[8 * g : 8 * g + 8], pltpu.roll(spare, 96 - 32 * g, 1))
            give[index, g] = tile
            got[mine, g] = tile
        for offset in PLANE:
            put(give.at[index], got.at[mine], red_send.at[index, 0], red_recv.at[index, 0], offset)

    def line_send(plane, got, mid, index):
        take(plane.at[0:15], red_recv.at[index, 0])
        value = plane[0]
        for i in range(1, 16):
            value = value + plane[i]
        mid[0] = value
        got[chip] = value
        for offset in LINE:
            put(mid.at[0], got.at[chip], red_send.at[index, 1], red_recv.at[index, 1], offset)

    def pair_send(line, got, mid, index):
        take(line.at[0:7], red_recv.at[index, 1])
        value = line[0]
        for i in range(1, 8):
            value = value + line[i]
        mid[1] = value
        pltpu.make_async_remote_copy(
            src_ref=mid.at[1], dst_ref=got, send_sem=red_send.at[index, 2], recv_sem=red_recv.at[index, 2],
            device_id=(gx + 1 - 2 * lax.rem(gx, 2), gy, gz), device_id_type=MESH,
        ).start()

    def pair_take(got, mid, index):
        take(got, red_recv.at[index, 2])
        tiles = [mid[1, g] + got[g] for g in range(3)]
        spare = jnp.zeros((8, 128), F32)
        for g in range(3):
            spare = jnp.where(lane8 // 32 == g, pltpu.roll(tiles[g], (32 + 32 * g) % 128, 1), spare)
        tiles = [jnp.where(lane8 < 96, tile, 0.0) for tile in tiles]
        return jnp.concatenate(tiles + [spare], axis=0)

    def field_rows(ref, i, count, inner):
        o = 1 if inner else 0
        return jnp.concatenate([ref[x + o, count * i + j + o] for j in range(count) for x in range(CX)], axis=1)

    for chunk in range(2):
        arrived(0, chunk)
        operate(0, chunk)
        send_near(1, chunk)

    def gram_zero(i, acc):
        v0 = field_rows(f1, i, GRAM, True)
        return acc + mm_nt(v0, v0)

    m0 = lax.fori_loop(0, CY // GRAM, gram_zero, jnp.zeros((NRHS, NRHS), F32))
    for chunk in range(2):
        arrived(1, chunk)
        operate(1, chunk)
        send_near(2, chunk)

    def gram_first(i, acc):
        v0, u1 = field_rows(f1, i, GRAM, True), field_rows(f2, i, GRAM, True)
        return acc + mm_nt(u1, jnp.concatenate([v0, u1], axis=0))

    first = lax.fori_loop(0, CY // GRAM, gram_first, jnp.zeros((NRHS, 64), F32))
    first = jnp.concatenate([m0, first, jnp.zeros((NRHS, 32), F32)], axis=1)
    lane32 = lanes((NRHS, 128))
    plane_send(first, plane_a, 0)

    for chunk in range(2):
        arrived(2, chunk)
        operate(2, chunk)
        send_near(3, chunk)
    line_send(plane_a, line_a, mid_a, 0)
    for chunk in range(2):
        arrived(3, chunk)
        operate(3, chunk)
    pair_send(line_a, pair_a, mid_a, 0)
    sums = pair_take(pair_a, mid_a, 0)

    solved, inverse = eliminate([pltpu.roll(sums, 96, 1), sums])
    alpha0 = part(solved, 3)
    turn0 = mm(part(solved, 1), alpha0)
    eye = jnp.where(sublanes((NRHS, NRHS)) == lanes((NRHS, NRHS)), 1.0, 0.0)
    beta0 = turn0 - eye
    rho1 = mm(part(sums, 0), beta0)
    back0 = mm(part(inverse, 1), beta0)
    mix = jnp.concatenate([turn0, -alpha0], axis=0).T

    def second_block(i, acc):
        v0, u1 = field_rows(f1, i, SECOND, True), field_rows(f2, i, SECOND, True)
        u2, u3 = field_rows(f3, i, SECOND, True), field_rows(f4, i, SECOND, False)
        top = jnp.concatenate([v0, u1, u2], axis=1)
        low = jnp.concatenate([u1, u2, u3], axis=1)
        new = mm(mix, jnp.concatenate([top, low], axis=0))
        n = 256 * SECOND
        p1, q1, aq1 = new[:, :n], new[:, n : 2 * n], new[:, 2 * n :]
        for j in range(SECOND):
            dirs[SECOND * i + j] = p1[:, 256 * j : 256 * j + 256]
            image[SECOND * i + j] = q1[:, 256 * j : 256 * j + 256]
        return acc + mm_nt(q1, jnp.concatenate([p1, q1, aq1], axis=0))

    grams = lax.fori_loop(0, CY // SECOND, second_block, jnp.zeros((NRHS, 96), F32))
    grams = jnp.concatenate([grams, jnp.zeros((NRHS, 32), F32)], axis=1)
    plane_send(grams, plane_b, 1)
    line_send(plane_b, line_b, mid_b, 1)
    pair_send(line_b, pair_b, mid_b, 1)
    sums = pair_take(pair_b, mid_b, 1)

    wide_rho = jnp.concatenate([rho1, jnp.zeros((NRHS, 96), F32)], axis=1)
    solved = eliminate([jnp.where(lane32 < 64, sums, pltpu.roll(wide_rho, 64, 1))])[0]
    alpha1 = part(solved, 2)
    turn1 = mm(part(solved, 1), alpha1)
    gram1, qq, qaq = part(sums, 0), part(sums, 1), part(sums, 2)
    gram2 = mm_t(alpha1, mm(qaq, alpha1) - mm(gram1, back0) - mm(qq, turn1))
    rho2 = mm(rho1, turn1 - eye)
    solved = eliminate([jnp.concatenate([gram2, rho2, jnp.zeros((NRHS, 64), F32)], axis=1)])[0]
    alpha2 = part(solved, 1)
    last = jnp.concatenate(
        [alpha0 - mm(beta0, alpha2), alpha1 + mm(turn1, alpha2), -mm(alpha1, alpha2)], axis=0
    ).T

    def finish(i, carry):
        old = [field_rows(f1, i, FINISH, True)]
        old += [jnp.concatenate([ref[FINISH * i + j] for j in range(FINISH)], axis=1) for ref in (dirs, image)]
        update = mm_three(last, jnp.concatenate(old, axis=0))
        for j in range(FINISH):
            for x in range(CX):
                piece = update[:, 128 * (2 * j + x) : 128 * (2 * j + x) + 128]
                value = f0[x + 1, FINISH * i + j + 1] + piece
                out_ref[pl.ds(CY * x + FINISH * i + j, NRHS, stride=CELLS), :] = value
        return carry

    lax.fori_loop(0, CY // FINISH, finish, 0)

    take(dummy.at[pl.ds(0, LABEL_TILES)], label_sem.at[0])
    for level in range(4):
        for chunk in range(2):
            take(dummy, halo_send.at[level, chunk])
    for index, (plane, line, pair) in enumerate(((plane_a, line_a, pair_a), (plane_b, line_b, pair_b))):
        take(plane.at[0:15], red_send.at[index, 0])
        take(line.at[0:7], red_send.at[index, 1])
        take(pair, red_send.at[index, 2])


def per_device(x_start, labels, conduct, electrodes):
    vmem = pl.BlockSpec(memory_space=pltpu.VMEM)
    field = pltpu.VMEM((CX + 2, CY + 2, NRHS, 128), F32)
    half = pltpu.VMEM((CY, NRHS, 256), F32)
    pack = pltpu.VMEM((2, 8, 128), F32)
    got = pltpu.VMEM((10, 2, 8, 128), F32)
    reduce = [
        pltpu.VMEM((16, 3, 8, 128), F32),
        pltpu.VMEM((8, 3, 8, 128), F32),
        pltpu.VMEM((3, 8, 128), F32),
        pltpu.VMEM((2, 3, 8, 128), F32),
        pltpu.VMEM((3, 8, 128), F32),
    ]
    out = pl.pallas_call(
        kernel,
        out_shape=jax.ShapeDtypeStruct((NRHS * CELLS, 128), F32),
        in_specs=[pl.BlockSpec(memory_space=pltpu.HBM)] * 4,
        out_specs=vmem,
        scratch_shapes=[
            pltpu.VMEM((NRHS * CELLS, 128), F32),
            pltpu.VMEM((CX, CY, 128), jnp.int32),
            pltpu.SMEM((LABELS, 9), F32),
            pltpu.SMEM((NRHS + 1,), jnp.int32),
            pltpu.SemaphoreType.DMA((4,)),
        ]
        + [field] * 4
        + [pltpu.VMEM((CX, CY, NRHS, 128), F32), half, half]
        + [
            pltpu.VMEM((18, CX, CY, 128), jnp.int32),
            pltpu.VMEM((3, CX + 2, 32, 128), jnp.int32),
            pltpu.VMEM((19, CELLS, 128), F32),
            pltpu.VMEM((19, CELLS, 8, 128), F32),
            pltpu.VMEM((5, 8, 128), F32),
        ]
        + [pack] * 4
        + [got] * 4
        + [pltpu.VMEM((2, 3, 8, 128), F32)]
        + reduce * 2
        + [
            pltpu.VMEM((HALO_TILES, 8, 128), F32),
            pltpu.SemaphoreType.DMA((4, 2)),
            pltpu.SemaphoreType.DMA((4, 2)),
            pltpu.SemaphoreType.DMA((2,)),
            pltpu.SemaphoreType.DMA((2, 3)),
            pltpu.SemaphoreType.DMA((2, 3)),
        ],
        compiler_params=pltpu.CompilerParams(
            collective_id=0, has_side_effects=True, vmem_limit_bytes=48 * 2**20
        ),
    )(x_start.reshape(NRHS * CELLS, 128), labels, conduct, electrodes)
    return out.reshape(x_start.shape)


def solution(mesh):
    return jax.shard_map(
        per_device,
        mesh=mesh,
        in_specs=(P(None, "gx", "gy", "gz"), P("gx", "gy", "gz"), P(), P()),
        out_specs=P(None, "gx", "gy", "gz"),
        check_vma=False,
    )
```
